256 devices in a mesh: pts: 64 (over z, y, core), cent: 4 (over x).
Axes of the slice: x: 4, y: 4, z: 8, core: 2. Of those that a mesh axis runs over, the one named last changes fastest.
Arguments:
- points: bfloat16 [524288, 512], P(('pts', 'cent')), may hold values from -128 to 128
- centroids: bfloat16 [65536, 512], P('pts'), may hold values from -32 to 32
- candidates: int32 [32768, 2], P(('pts', 'cent')), may hold values from 0 to 255, all different within a row; in each aligned block of 128 rows (0 to 127, 128 to 255, ...) at most 2 rows name the same one
Outputs:
- new_centroids: bfloat16 [65536, 512], P('pts')
- point_lse: float32 [524288], P(('pts', 'cent'))
The draws below stay inside these ranges and needn't reach their ends.
Inputs may be any that keep to these rules, and one draw needn't show every extreme that they name: `candidates`: within the 128 point blocks of one device, no centroid block is named more than 2 times; the two ids of a point block differ.
All inputs are finite; a program needn't handle non-finite values.
Results may differ from the reference program's by a relative error of at most 0.006.
Values may be sent and summed in bfloat16 or wider, within the bound.
No kernel may reach another device: no remote copies, remote signals or barrier semaphores. Data moves between devices by JAX's collectives and lax.ppermute only.
A program may use at most 64 MiB of HBM per device.

```python
import math
import jax
import jax.numpy as jnp
import numpy as np
from jax import lax

D = 512
CB = 256
PB = 16
PBD = 128
ITERS = 2
NCB = 256
K = 65536
CAP = 2
NPB = 32768
NPTS = 524288


def draw_centroids(key, part):
    values = jnp.clip(jax.random.normal(jax.random.fold_in(key, 11), (K, D), jnp.float32), -6.0, 6.0)
    return jnp.clip(values, -32.0, 32.0).astype(jnp.bfloat16)


def draw_points(key, part):
    values = jnp.clip(jax.random.normal(jax.random.fold_in(key, 17), (NPTS, D), jnp.float32), -6.0, 6.0)
    return jnp.clip(values, -128.0, 128.0).astype(jnp.bfloat16)


def deal_out(rng, own, number, rows, amount, top, reach, skew):
    ranking = jax.random.permutation(rng, amount)
    heavy_load, ordinary = shares(amount, rows * top, reach, skew, True), shares(amount, rows * top, reach, skew, False)
    places = jnp.arange(amount)

    def named(tallies, turn):
        used = int((tallies > 0).sum())
        fixed = max(1, used // 4)
        passed = fixed + (places - fixed + turn * (used - fixed)) % max(1, amount - fixed)
        return jnp.zeros((amount,), jnp.int32).at[ranking[jnp.where(places < fixed, places, passed)]].set(jnp.asarray(tallies, jnp.int32))

    tallies = jnp.where(number % 4 == 0, named(heavy_load, number // 4), named(ordinary, number - number // 4 - 1))
    mixed = jax.random.permutation(jax.random.fold_in(own, 3), amount)
    donor, receiver = mixed[0:amount // 2 * 2:2], mixed[1:amount // 2 * 2:2]
    room = jnp.minimum(tallies[donor] - 1, reach - tallies[receiver]) // 2
    room = jnp.where((donor == ranking[0]) | (receiver == ranking[0]) | (tallies[receiver] == 0), 0, jnp.maximum(room, 0))
    passed = jax.random.randint(jax.random.fold_in(own, 4), (amount // 2,), 0, 1 << 20) % (room + 1)
    tallies = tallies.at[donor].add(-passed).at[receiver].add(passed)
    items = jnp.searchsorted(jnp.cumsum(tallies), jnp.arange(rows * top), side="right").astype(jnp.int32)
    grid = items.reshape(top, rows).T
    grid = grid[jax.random.permutation(jax.random.fold_in(own, 1), rows)]
    turn = jax.random.randint(jax.random.fold_in(own, 2), (rows, 1), 0, top)
    return jnp.take_along_axis(grid, (jnp.arange(top)[None, :] + turn) % top, axis=1)


def shares(number_of, total, limit, lean, full):
    loads = [(1 << 20) // math.isqrt(standing ** lean) + 1 for standing in range(1, number_of + 1)]
    largest = limit if full else min(limit, max(-(-total // number_of), total * loads[0] // sum(loads)))
    least = 1 if total - largest >= number_of - 1 else 0
    holding, surplus = [largest] + [least] * (number_of - 1), total - largest - least * (number_of - 1)
    while surplus > 0:
        free = [i for i in range(1, number_of) if holding[i] < largest] or [i for i in range(1, number_of) if holding[i] < limit]
        pool, budget = sum([loads[i] for i in free]), surplus
        for i in free:
            extra = min(limit - holding[i], max(1, budget * loads[i] // pool), surplus)
            holding[i] = holding[i] + extra
            surplus = surplus - extra
    return np.array(holding)


def setup_inputs(seed: int = 0) -> dict:
    key_list = jax.random.split(jax.random.key(seed), 4)
    points = draw_points(jax.random.fold_in(key_list[3], 71), 0)
    centroids = draw_centroids(jax.random.fold_in(key_list[3], 71), 0)
    candidates_keys = jax.random.split(jax.random.fold_in(key_list[2], 1), NPB // PBD)
    candidates_turns = jax.random.permutation(jax.random.fold_in(key_list[2], 3), NPB // PBD)
    candidates = jax.vmap(lambda own, number: deal_out(jax.random.fold_in(key_list[2], 2), own, number, PBD, NCB, 2, CAP, 2))(candidates_keys, candidates_turns).reshape((NPB, 2))
    return dict(points=points, centroids=centroids, candidates=candidates)


def stable_lse(scores, reduce_axis):
    highest = lax.optimization_barrier(jnp.max(scores, axis=reduce_axis, keepdims=True))
    summed = lax.optimization_barrier(jnp.sum(jnp.exp(scores - highest), axis=reduce_axis))
    return jnp.squeeze(highest, reduce_axis) + jnp.log(summed)

def em_round(points, current, candidates):
    inverse_root = 1.0 / math.sqrt(D)
    group_count = candidates.shape[0] // PBD
    grouped = points.reshape(group_count, PBD, PB, D)
    picked = candidates.reshape(group_count, PBD, 2)
    centre_table = current.reshape(NCB, CB, D)
    centre_norms = lax.optimization_barrier(jnp.sum(jnp.square(centre_table.astype(jnp.float32)), axis=2))

    def visit_group(running, element):
        weighted, masses = running
        group_rows, group_ids = element
        chosen = centre_table[group_ids].astype(jnp.float32)
        products = jnp.einsum('gpd,gjmd->gjpm', group_rows.astype(jnp.float32), chosen)
        scores = inverse_root * (2.0 * products - centre_norms[group_ids][:, :, None, :])
        partial_value = stable_lse(scores, 3)
        point_lse = stable_lse(partial_value, 1)
        weights = jnp.exp(scores - point_lse[:, None, :, None])
        rounded = lax.optimization_barrier(weights.astype(jnp.bfloat16)).astype(jnp.float32)
        contribution = jnp.einsum('gjpm,gpd->gjmd', rounded, group_rows.astype(jnp.float32))
        weighted = weighted.at[group_ids].add(contribution)
        masses = masses.at[group_ids].add(lax.optimization_barrier(jnp.sum(weights, axis=2)))
        return ((weighted, masses), point_lse)
    start_sums = jnp.zeros((NCB, CB, D), jnp.float32)
    start_mass = jnp.zeros((NCB, CB), jnp.float32)
    (weighted, masses), point_lse = lax.scan(visit_group, (start_sums, start_mass), (grouped, picked))
    return (weighted.reshape(K, D), masses.reshape(K), point_lse.reshape(-1))

def reference(points, centroids, candidates):
    current = centroids
    point_lse = jnp.zeros((NPTS,), jnp.float32)
    for iteration in range(ITERS):
        weighted, masses, point_lse = em_round(points, current, candidates)
        current = ((weighted + current.astype(jnp.float32)) / (masses[:, None] + 1.0)).astype(jnp.bfloat16)
    return (current, point_lse)
```

```python
import functools
import math

import jax
import jax.numpy as jnp
from jax import lax
from jax.experimental import pallas as pl
from jax.experimental.pallas import tpu as pltpu
from jax.sharding import Mesh, PartitionSpec as P

D = 512
CB = 256
PB = 16
PBD = 128
NCB = 256
ITERS = 2
CAP = 2
COPIES = 4
PEERS = NCB // COPIES
LANES = COPIES * CAP * PB
SLOTS = PEERS * COPIES * CAP
ENTRIES = 2 * PBD
STEP = 16
COLS = STEP * CAP * PB
MSG = CB + 16
EMPTY = 1e30
GROUP = ("zl", "y", "core", "x")
BETA = 1.0 / math.sqrt(D)
F32 = jnp.float32
BF16 = jnp.bfloat16


def exact_dot(a, b):
    return jnp.dot(a, b, precision=lax.Precision.HIGHEST, preferred_element_type=F32)


def iota(shape, dim):
    return lax.broadcasted_iota(jnp.int32, shape, dim)


def pack_kernel(src, points, out):
    base = pl.program_id(0) * out.shape[0]

    def body(i, carry):
        s = src[base + i]
        block = points[jnp.maximum(s, 0)]
        out[i] = jnp.where(s >= 0, block, jnp.zeros_like(block))
        return carry

    lax.fori_loop(0, out.shape[0], body, 0, unroll=8)


def pack(src, points):
    per = 64
    return pl.pallas_call(
        pack_kernel,
        grid_spec=pltpu.PrefetchScalarGridSpec(
            num_scalar_prefetch=1,
            grid=(SLOTS // per,),
            in_specs=[pl.BlockSpec((PBD, PB, D), lambda i, s: (0, 0, 0))],
            out_specs=pl.BlockSpec((per, PB, D), lambda i, s: (i, 0, 0)),
        ),
        out_shape=jax.ShapeDtypeStruct((SLOTS, PB, D), BF16),
        compiler_params=pltpu.CompilerParams(vmem_limit_bytes=16 << 20),
        name="pack_points",
    )(src, points)


def rows_of(rows, label):
    part = rows[:, pl.ds(pl.multiple_of(label * (CAP * PB), CAP * PB), CAP * PB), :]
    return part.reshape(COLS, D)


def norms_of(table):
    wide = table[...].astype(F32)
    return jnp.sum(wide * wide, axis=1, keepdims=True)


def scores_of(table, block, norms):
    products = lax.dot_general(table[...], block, (((1,), (1,)), ((), ())), preferred_element_type=F32)
    return BETA * (2.0 * products - norms)


def label_of(me, s):
    return lax.rem(me + 1 + s, COPIES)


def score_kernel(me, rows, c0, c1, c2, c3, out, norms):
    tables = (c0, c1, c2, c3)

    @pl.when(pl.program_id(0) == 0)
    def _():
        for s in range(COPIES):
            norms[s] = jnp.broadcast_to(norms_of(tables[s]), (CB, 128))

    own = iota((STEP, COLS), 1) // (CAP * PB) == iota((STEP, COLS), 0)
    fold_from, fold_to = iota((COLS, LANES), 0), iota((COLS, LANES), 1)
    total = jnp.zeros((STEP, LANES), F32)
    for s in range(COPIES):
        label = label_of(me[0], s)
        scores = scores_of(tables[s], rows_of(rows, label), norms[s][:, :1])
        highest = jnp.max(scores, axis=0, keepdims=True)
        partial = highest + jnp.log(jnp.sum(jnp.exp(scores - highest), axis=0, keepdims=True))
        fold = fold_from % (CAP * PB) + label * (CAP * PB) == fold_to
        total += exact_dot(jnp.where(own, partial, 0.0), fold.astype(F32))
    out[...] = total


def table_specs():
    return [pl.BlockSpec((CB, D), lambda i, s: (0, 0))] * COPIES


def row_spec():
    return pl.BlockSpec((STEP, LANES, D), lambda i, s: (i, 0, 0))


def score(me, rows, tables):
    return pl.pallas_call(
        score_kernel,
        grid_spec=pltpu.PrefetchScalarGridSpec(
            num_scalar_prefetch=1,
            grid=(PEERS // STEP,),
            in_specs=[row_spec(), *table_specs()],
            out_specs=pl.BlockSpec((STEP, LANES), lambda i, s: (i, 0)),
            scratch_shapes=[pltpu.VMEM((COPIES, CB, 128), F32)],
        ),
        out_shape=jax.ShapeDtypeStruct((PEERS, LANES), F32),
        compiler_params=pltpu.CompilerParams(vmem_limit_bytes=40 << 20),
        name="score_blocks",
    )(me, rows, *tables)


def home_kernel(returned, peer_col, slot_col, peer_row, lse, outward):
    pick = (iota((ENTRIES, PEERS), 1) == peer_col[...]).astype(F32)
    mask = (iota((ENTRIES, LANES), 1) // PB == slot_col[...]).astype(F32)
    fold = (iota((LANES, LANES), 0) % PB == iota((LANES, LANES), 1) % PB).astype(F32)
    mine = exact_dot(exact_dot(pick, returned[...]) * mask, fold)
    first, second = mine[:PBD], mine[PBD:]
    highest = jnp.maximum(first, second)
    total = highest + jnp.log(jnp.exp(first - highest) + jnp.exp(second - highest))
    lse[...] = total
    place = (iota((PEERS, ENTRIES), 0) == peer_row[...]).astype(F32)
    filled = jnp.dot(place.astype(BF16), mask.astype(BF16), preferred_element_type=F32)
    both = jnp.concatenate([total, total], axis=0)
    outward[...] = jnp.where(filled > 0.5, exact_dot(place, both * mask), EMPTY)


def home(returned, peer_col, slot_col, peer_row):
    return pl.pallas_call(
        home_kernel,
        out_shape=(
            jax.ShapeDtypeStruct((PBD, LANES), F32),
            jax.ShapeDtypeStruct((PEERS, LANES), F32),
        ),
        name="join_halves",
    )(returned, peer_col, slot_col, peer_row)


def weigh_kernel(me, rows, c0, c1, c2, c3, inward, message, own_sum, own_mass, norms, sums, masses):
    tables = (c0, c1, c2, c3)

    @pl.when(pl.program_id(0) == 0)
    def _():
        for s in range(COPIES):
            norms[s] = jnp.broadcast_to(norms_of(tables[s]), (CB, 128))
        sums[...] = jnp.zeros_like(sums)
        masses[...] = jnp.zeros_like(masses)

    own = iota((STEP, COLS), 1) // (CAP * PB) == iota((STEP, COLS), 0)
    spread_from, spread_to = iota((LANES, COLS), 0), iota((LANES, COLS), 1)
    for s in range(COPIES):
        label = label_of(me[0], s)
        block = rows_of(rows, label)
        spread = spread_to % (CAP * PB) + label * (CAP * PB) == spread_from
        point_lse = exact_dot(inward[...], spread.astype(F32))
        point_lse = jnp.sum(jnp.where(own, point_lse, 0.0), axis=0, keepdims=True)
        weights = jnp.exp(scores_of(tables[s], block, norms[s][:, :1]) - point_lse)
        sums[s] += jnp.dot(weights.astype(BF16), block, preferred_element_type=F32)
        mass = weights[:, :128]
        for k in range(1, COLS // 128):
            mass += weights[:, k * 128 : (k + 1) * 128]
        masses[s] += mass

    @pl.when(pl.program_id(0) == pl.num_programs(0) - 1)
    def _():
        for s in range(COPIES):
            mass = jnp.sum(masses[s].T, axis=0, keepdims=True)
            if s == COPIES - 1:
                own_sum[...] = sums[s]
                own_mass[...] = jnp.broadcast_to(mass, own_mass.shape)
            else:
                message[s, :CB] = sums[s].astype(BF16)
                coarse = mass.astype(BF16)
                fine = (mass - coarse.astype(F32)).astype(BF16)
                pair = jnp.concatenate([coarse.astype(F32), fine.astype(F32)], axis=1)
                message[s, CB:] = jnp.broadcast_to(pair, (MSG - CB, D)).astype(BF16)


def weigh(me, rows, tables, inward):
    whole = lambda *shape: pl.BlockSpec(shape, lambda i, s: (0,) * len(shape))
    return pl.pallas_call(
        weigh_kernel,
        grid_spec=pltpu.PrefetchScalarGridSpec(
            num_scalar_prefetch=1,
            grid=(PEERS // STEP,),
            in_specs=[row_spec(), *table_specs(), pl.BlockSpec((STEP, LANES), lambda i, s: (i, 0))],
            out_specs=[whole(COPIES - 1, MSG, D), whole(CB, D), whole(8, CB)],
            scratch_shapes=[
                pltpu.VMEM((COPIES, CB, 128), F32),
                pltpu.VMEM((COPIES, CB, D), F32),
                pltpu.VMEM((COPIES, CB, 128), F32),
            ],
        ),
        out_shape=(
            jax.ShapeDtypeStruct((COPIES - 1, MSG, D), BF16),
            jax.ShapeDtypeStruct((CB, D), F32),
            jax.ShapeDtypeStruct((8, CB), F32),
        ),
        compiler_params=pltpu.CompilerParams(vmem_limit_bytes=40 << 20),
        name="weigh_points",
    )(me, rows, *tables, inward)


def finish_kernel(own_sum, own_mass, m0, m1, m2, table, out):
    total, mass = own_sum[...], own_mass[:1]
    for message in (m0, m1, m2):
        total += message[:CB].astype(F32)
        pair = message[CB:].astype(F32)[:1]
        mass += pair[:, :CB] + pair[:, CB:]
    column = jnp.broadcast_to(mass + 1.0, (128, CB)).T[:, :1]
    fresh = ((total + table[...].astype(F32)) / column).astype(BF16)
    out[...] = jnp.broadcast_to(fresh, out.shape)


def finish(own_sum, own_mass, arrived, table, copies):
    return pl.pallas_call(
        finish_kernel,
        out_shape=jax.ShapeDtypeStruct((*copies, CB, D), BF16),
        compiler_params=pltpu.CompilerParams(vmem_limit_bytes=16 << 20),
        name="new_centres",
    )(own_sum, own_mass, *arrived, table)


def shifted(value, by):
    return lax.ppermute(value, "zh", [(i, (i + by) % COPIES) for i in range(COPIES)])


def tables_of(own):
    return [shifted(own, COPIES - 1 - s) for s in range(COPIES - 1)] + [own]


def exchange(value):
    return lax.all_to_all(value, GROUP, split_axis=0, concat_axis=0, tiled=True)


def route(candidates):
    picked = candidates.T.reshape(-1)
    labels = jnp.arange(NCB, dtype=jnp.int32)
    member = (picked[:, None] == labels[None, :]).astype(BF16)
    index = jnp.arange(ENTRIES, dtype=jnp.int32)
    earlier = (index[None, :] < index[:, None]).astype(BF16)
    hits = jnp.dot(earlier, member, preferred_element_type=F32)
    arrival = jnp.sum(hits * member.astype(F32), axis=1).astype(jnp.int32)
    peer = picked % PEERS
    slot = picked // PEERS * CAP + arrival
    position = peer * (COPIES * CAP) + slot
    places = jnp.arange(SLOTS, dtype=jnp.int32)
    source = jnp.sum(jnp.where(position[:, None] == places[None, :], index[:, None] % PBD + 1, 0), axis=0) - 1
    return source, peer, slot


def on_device(points, centroids, candidates):
    me = lax.axis_index("zh").reshape(1)
    own = lax.dynamic_slice_in_dim(centroids, lax.axis_index("x") * CB, CB, 0)
    source, peer, slot = route(candidates)
    outgoing = pack(source, points.reshape(PBD, PB, D))
    tables = tables_of(own)
    rows = exchange(outgoing.reshape(PEERS, LANES, D))
    for iteration in range(ITERS):
        returned = exchange(score(me, rows, tables))
        lse, outward = home(returned, peer[:, None], slot[:, None], peer[None, :])
        message, own_sum, own_mass = weigh(me, rows, tables, exchange(outward))
        arrived = [shifted(message[n - 1], n) for n in range(1, COPIES)]
        last = iteration == ITERS - 1
        own = finish(own_sum, own_mass, arrived, own, (COPIES,) if last else ())
        if not last:
            tables = tables_of(own)
    gathered = lax.all_to_all(own, "x", split_axis=0, concat_axis=0, tiled=True)
    return gathered.reshape(COPIES * CB, D), lse[:, :PB].reshape(-1)


def solution(mesh):
    split = Mesh(mesh.devices.reshape(4, 2, 4, 2, 4), ("zh", "zl", "y", "core", "x"))
    pts = ("zh", "zl", "y", "core")
    return jax.shard_map(
        on_device,
        mesh=split,
        in_specs=(P((*pts, "x"), None), P(pts, None), P((*pts, "x"), None)),
        out_specs=(P(pts, None), P((*pts, "x"))),
        check_vma=False,
    )
```

```python
import functools
import math

import jax
import jax.numpy as jnp
from jax import lax
from jax.experimental import pallas as pl
from jax.experimental.pallas import tpu as pltpu
from jax.sharding import Mesh, PartitionSpec as P

D = 512
CB = 256
PB = 16
PBD = 128
NCB = 256
ITERS = 2
CAP = 2
COPIES = 4
PEERS = NCB // COPIES
LANES = COPIES * CAP * PB
SLOTS = PEERS * COPIES * CAP
ENTRIES = 2 * PBD
STEP = 64
COLS = STEP * CAP * PB
MSG = CB + 16
EMPTY = 1e30
GROUP = ("zl", "y", "core", "x")
BETA = 1.0 / math.sqrt(D)
LOG2E = 1.0 / math.log(2.0)
LN2 = math.log(2.0)
F32 = jnp.float32
BF16 = jnp.bfloat16


def exact_dot(a, b):
    return jnp.dot(a, b, precision=lax.Precision.HIGHEST, preferred_element_type=F32)


def iota(shape, dim):
    return lax.broadcasted_iota(jnp.int32, shape, dim)


def pack_kernel(src, points, out):
    base = pl.program_id(0) * out.shape[0]

    def body(i, carry):
        s = src[base + i]
        block = points[jnp.maximum(s, 0)]
        out[i] = jnp.where(s >= 0, block, jnp.zeros_like(block))
        return carry

    lax.fori_loop(0, out.shape[0], body, 0, unroll=8)


def pack(src, points):
    per = 128
    return pl.pallas_call(
        pack_kernel,
        grid_spec=pltpu.PrefetchScalarGridSpec(
            num_scalar_prefetch=1,
            grid=(SLOTS // per,),
            in_specs=[pl.BlockSpec((PBD, PB, D), lambda i, s: (0, 0, 0))],
            out_specs=pl.BlockSpec((per, PB, D), lambda i, s: (i, 0, 0)),
        ),
        out_shape=jax.ShapeDtypeStruct((SLOTS, PB, D), BF16),
        compiler_params=pltpu.CompilerParams(vmem_limit_bytes=20 << 20),
        name="pack_points",
    )(src, points)


def rows_of(rows, label):
    part = rows[:, pl.ds(pl.multiple_of(label * (CAP * PB), CAP * PB), CAP * PB), :]
    return part.reshape(COLS, D)


def norms_of(table):
    wide = table[...].astype(F32)
    return (BETA * LOG2E) * jnp.sum(wide * wide, axis=1, keepdims=True)


def scores_of(table, block, norms):
    products = lax.dot_general(table[...], block, (((1,), (1,)), ((), ())), preferred_element_type=F32)
    return (2.0 * BETA * LOG2E) * products - norms


def turned_by(value, groups, per_row):
    row = iota(value.shape, 0) % COPIES
    turned = value
    for k in range(COPIES):
        turn = lax.rem(groups + per_row * k + 2 * COPIES, COPIES) * (CAP * PB)
        turned = jnp.where(row == k, pltpu.roll(value, turn, 1), turned)
    return turned


def label_of(me, s):
    return lax.rem(me + 1 + s, COPIES)


def score_kernel(me, rows, c0, c1, c2, c3, out, norms):
    tables = (c0, c1, c2, c3)

    @pl.when(pl.program_id(0) == 0)
    def _():
        for s in range(COPIES):
            norms[s] = jnp.broadcast_to(norms_of(tables[s]), (CB, 128))

    lanes = iota((STEP, LANES), 1) // (CAP * PB)
    total = jnp.zeros((STEP, LANES), F32)
    for s in range(COPIES):
        label = label_of(me[0], s)
        scores = scores_of(tables[s], rows_of(rows, label), norms[s][:, :1])
        highest = jnp.max(scores, axis=0, keepdims=True)
        partial = highest + jnp.log2(jnp.sum(jnp.exp2(scores - highest), axis=0, keepdims=True))
        partial = partial * LN2
        tiles = [jnp.broadcast_to(partial[:, k : k + LANES], (COPIES, LANES)) for k in range(0, COLS, LANES)]
        total = jnp.where(lanes == label, turned_by(jnp.concatenate(tiles, axis=0), label, -1), total)
    out[...] = total


def table_specs():
    return [pl.BlockSpec((CB, D), lambda i, s: (0, 0))] * COPIES


def row_spec():
    return pl.BlockSpec((STEP, LANES, D), lambda i, s: (i, 0, 0))


def score(me, rows, tables):
    return pl.pallas_call(
        score_kernel,
        grid_spec=pltpu.PrefetchScalarGridSpec(
            num_scalar_prefetch=1,
            grid=(PEERS // STEP,),
            in_specs=[row_spec(), *table_specs()],
            out_specs=pl.BlockSpec((STEP, LANES), lambda i, s: (i, 0)),
            scratch_shapes=[pltpu.VMEM((COPIES, CB, 128), F32)],
        ),
        out_shape=jax.ShapeDtypeStruct((PEERS, LANES), F32),
        compiler_params=pltpu.CompilerParams(vmem_limit_bytes=40 << 20),
        name="score_blocks",
    )(me, rows, *tables)


def home_kernel(returned, peer_col, slot_col, peer_row, lse, outward):
    pick = (iota((ENTRIES, PEERS), 1) == peer_col[...]).astype(F32)
    mask = (iota((ENTRIES, LANES), 1) // PB == slot_col[...]).astype(F32)
    fold = (iota((LANES, LANES), 0) % PB == iota((LANES, LANES), 1) % PB).astype(F32)
    mine = exact_dot(exact_dot(pick, returned[...]) * mask, fold)
    first, second = mine[:PBD], mine[PBD:]
    highest = jnp.maximum(first, second)
    total = highest + jnp.log(jnp.exp(first - highest) + jnp.exp(second - highest))
    lse[...] = total
    place = (iota((PEERS, ENTRIES), 0) == peer_row[...]).astype(F32)
    filled = jnp.dot(place.astype(BF16), mask.astype(BF16), preferred_element_type=F32)
    both = jnp.concatenate([total, total], axis=0)
    outward[...] = jnp.where(filled > 0.5, exact_dot(place, both * mask), EMPTY)


def home(returned, peer_col, slot_col, peer_row):
    return pl.pallas_call(
        home_kernel,
        out_shape=(
            jax.ShapeDtypeStruct((PBD, LANES), F32),
            jax.ShapeDtypeStruct((PEERS, LANES), F32),
        ),
        name="join_halves",
    )(returned, peer_col, slot_col, peer_row)


def weigh_kernel(me, rows, c0, c1, c2, c3, inward, message, own_sum, own_mass, norms, sums, masses):
    tables = (c0, c1, c2, c3)

    @pl.when(pl.program_id(0) == 0)
    def _():
        for s in range(COPIES):
            norms[s] = jnp.broadcast_to(norms_of(tables[s]), (CB, 128))
        sums[...] = jnp.zeros_like(sums)
        masses[...] = jnp.zeros_like(masses)

    mine = iota((STEP, LANES), 1) // (CAP * PB) == iota((STEP, LANES), 0) % COPIES
    incoming = inward[...] * LOG2E
    for s in range(COPIES):
        label = label_of(me[0], s)
        block = rows_of(rows, label)
        turned = jnp.where(mine, turned_by(incoming, -label, 1), 0.0)
        tiles = [jnp.sum(turned[k : k + COPIES], axis=0, keepdims=True) for k in range(0, STEP, COPIES)]
        point_lse = jnp.concatenate(tiles, axis=1)
        weights = jnp.exp2(scores_of(tables[s], block, norms[s][:, :1]) - point_lse)
        sums[s] += jnp.dot(weights.astype(BF16), block, preferred_element_type=F32)
        mass = weights[:, :128]
        for k in range(1, COLS // 128):
            mass += weights[:, k * 128 : (k + 1) * 128]
        masses[s] += mass

    @pl.when(pl.program_id(0) == pl.num_programs(0) - 1)
    def _():
        for s in range(COPIES):
            mass = jnp.sum(masses[s].T, axis=0, keepdims=True)
            if s == COPIES - 1:
                own_sum[...] = sums[s]
                own_mass[...] = jnp.broadcast_to(mass, own_mass.shape)
            else:
                message[s, :CB] = sums[s].astype(BF16)
                coarse = mass.astype(BF16)
                fine = (mass - coarse.astype(F32)).astype(BF16)
                pair = jnp.concatenate([coarse.astype(F32), fine.astype(F32)], axis=1)
                message[s, CB:] = jnp.broadcast_to(pair, (MSG - CB, D)).astype(BF16)


def weigh(me, rows, tables, inward):
    whole = lambda *shape: pl.BlockSpec(shape, lambda i, s: (0,) * len(shape))
    return pl.pallas_call(
        weigh_kernel,
        grid_spec=pltpu.PrefetchScalarGridSpec(
            num_scalar_prefetch=1,
            grid=(PEERS // STEP,),
            in_specs=[row_spec(), *table_specs(), pl.BlockSpec((STEP, LANES), lambda i, s: (i, 0))],
            out_specs=[whole(COPIES - 1, MSG, D), whole(CB, D), whole(8, CB)],
            scratch_shapes=[
                pltpu.VMEM((COPIES, CB, 128), F32),
                pltpu.VMEM((COPIES, CB, D), F32),
                pltpu.VMEM((COPIES, CB, 128), F32),
            ],
        ),
        out_shape=(
            jax.ShapeDtypeStruct((COPIES - 1, MSG, D), BF16),
            jax.ShapeDtypeStruct((CB, D), F32),
            jax.ShapeDtypeStruct((8, CB), F32),
        ),
        compiler_params=pltpu.CompilerParams(vmem_limit_bytes=40 << 20),
        name="weigh_points",
    )(me, rows, *tables, inward)


def finish_kernel(own_sum, own_mass, m0, m1, m2, table, out):
    total, mass = own_sum[...], own_mass[:1]
    for message in (m0, m1, m2):
        total += message[:CB].astype(F32)
        pair = message[CB:].astype(F32)[:1]
        mass += pair[:, :CB] + pair[:, CB:]
    column = jnp.broadcast_to(mass + 1.0, (128, CB)).T[:, :1]
    fresh = ((total + table[...].astype(F32)) / column).astype(BF16)
    out[...] = jnp.broadcast_to(fresh, out.shape)


def finish(own_sum, own_mass, arrived, table, copies):
    return pl.pallas_call(
        finish_kernel,
        out_shape=jax.ShapeDtypeStruct((*copies, CB, D), BF16),
        compiler_params=pltpu.CompilerParams(vmem_limit_bytes=16 << 20),
        name="new_centres",
    )(own_sum, own_mass, *arrived, table)


def shifted(value, by):
    return lax.ppermute(value, "zh", [(i, (i + by) % COPIES) for i in range(COPIES)])


def tables_of(own):
    return [shifted(own, COPIES - 1 - s) for s in range(COPIES - 1)] + [own]


def exchange(value):
    return lax.all_to_all(value, GROUP, split_axis=0, concat_axis=0, tiled=True)


def route(candidates):
    picked = candidates.T.reshape(-1)
    labels = jnp.arange(NCB, dtype=jnp.int32)
    member = (picked[:, None] == labels[None, :]).astype(BF16)
    index = jnp.arange(ENTRIES, dtype=jnp.int32)
    earlier = (index[None, :] < index[:, None]).astype(BF16)
    hits = jnp.dot(earlier, member, preferred_element_type=F32)
    arrival = jnp.sum(hits * member.astype(F32), axis=1).astype(jnp.int32)
    peer = picked % PEERS
    slot = picked // PEERS * CAP + arrival
    position = peer * (COPIES * CAP) + slot
    places = jnp.arange(SLOTS, dtype=jnp.int32)
    source = jnp.sum(jnp.where(position[:, None] == places[None, :], index[:, None] % PBD + 1, 0), axis=0) - 1
    return source, peer, slot


def on_device(points, centroids, candidates):
    me = lax.axis_index("zh").reshape(1)
    own = lax.dynamic_slice_in_dim(centroids, lax.axis_index("x") * CB, CB, 0)
    source, peer, slot = route(candidates)
    outgoing = pack(source, points.reshape(PBD, PB, D))
    outgoing, *tables = lax.optimization_barrier((outgoing, *tables_of(own)))
    rows = exchange(outgoing.reshape(PEERS, LANES, D))
    for iteration in range(ITERS):
        returned = exchange(score(me, rows, tables))
        lse, outward = home(returned, peer[:, None], slot[:, None], peer[None, :])
        message, own_sum, own_mass = weigh(me, rows, tables, exchange(outward))
        arrived = [shifted(message[n - 1], n) for n in range(1, COPIES)]
        last = iteration == ITERS - 1
        own = finish(own_sum, own_mass, arrived, own, (COPIES,) if last else ())
        if not last:
            tables = tables_of(own)
    gathered = lax.all_to_all(own, "x", split_axis=0, concat_axis=0, tiled=True)
    return gathered.reshape(COPIES * CB, D), lse[:, :PB].reshape(-1)


def solution(mesh):
    split = Mesh(mesh.devices.reshape(4, 2, 4, 2, 4), ("zh", "zl", "y", "core", "x"))
    pts = ("zh", "zl", "y", "core")
    return jax.shard_map(
        on_device,
        mesh=split,
        in_specs=(P((*pts, "x"), None), P(pts, None), P((*pts, "x"), None)),
        out_specs=(P(pts, None), P((*pts, "x"))),
        check_vma=False,
    )
```

```python
import functools
import math

import jax
import jax.numpy as jnp
from jax import lax
from jax.experimental import pallas as pl
from jax.experimental.pallas import tpu as pltpu
from jax.sharding import Mesh, PartitionSpec as P

D = 512
CB = 256
PB = 16
PBD = 128
NCB = 256
ITERS = 2
CAP = 2
COPIES = 4
PEERS = NCB // COPIES
LANES = COPIES * CAP * PB
SLOTS = PEERS * COPIES * CAP
ENTRIES = 2 * PBD
COLS = PEERS * CAP * PB
MSG = CB + 16
EMPTY = 1e30
GROUP = ("zl", "y", "core", "x")
BETA = 1.0 / math.sqrt(D)
LOG2E = 1.0 / math.log(2.0)
LN2 = math.log(2.0)
F32 = jnp.float32
BF16 = jnp.bfloat16


def picked_sum(chosen, values):
    total = None
    for _ in range(3):
        piece = values.astype(BF16)
        part = jnp.dot(chosen, piece, preferred_element_type=F32)
        total = part if total is None else total + part
        values = values - piece.astype(F32)
    return total


def iota(shape, dim):
    return lax.broadcasted_iota(jnp.int32, shape, dim)


def pack_kernel(src, points, out):
    base = pl.program_id(0) * out.shape[0]

    def body(i, carry):
        s = src[base + i]
        block = points[jnp.maximum(s, 0)]
        out[i] = jnp.where(s >= 0, block, jnp.zeros_like(block))
        return carry

    lax.fori_loop(0, out.shape[0], body, 0, unroll=8)


def pack(src, points):
    per = 128
    return pl.pallas_call(
        pack_kernel,
        grid_spec=pltpu.PrefetchScalarGridSpec(
            num_scalar_prefetch=1,
            grid=(SLOTS // per,),
            in_specs=[pl.BlockSpec((PBD, PB, D), lambda i, s: (0, 0, 0))],
            out_specs=pl.BlockSpec((per, PB, D), lambda i, s: (i, 0, 0)),
        ),
        out_shape=jax.ShapeDtypeStruct((SLOTS, PB, D), BF16),
        compiler_params=pltpu.CompilerParams(vmem_limit_bytes=20 << 20),
        name="pack_points",
    )(src, points)


def norms_of(table):
    wide = table[...].astype(F32)
    return (BETA * LOG2E) * jnp.sum(wide * wide, axis=1, keepdims=True)


def scores_of(table, block, norms):
    products = lax.dot_general(table[...], block, (((1,), (1,)), ((), ())), preferred_element_type=F32)
    return (2.0 * BETA * LOG2E) * products - norms


def turned_by(value, groups, per_row):
    row = iota(value.shape, 0) % COPIES
    turned = value
    for k in range(COPIES):
        turn = lax.rem(groups + per_row * k + 2 * COPIES, COPIES) * (CAP * PB)
        turned = jnp.where(row == k, pltpu.roll(value, turn, 1), turned)
    return turned


def label_of(me, s):
    return lax.rem(me + 1 + s, COPIES)


def each_label(which, body):
    for k in range(len(which)):
        pl.when(pl.program_id(0) == k)(functools.partial(body, k))


def call_by_label(kernel, me, rows, tables, which, extra, outs, out_specs, flops, name):
    first = which[0]
    by = which[1] - which[0] if len(which) > 1 else 0
    row_spec = pl.BlockSpec((PEERS, CAP * PB, D), lambda i, m: (0, label_of(m[0], first + by * i), 0))
    whole = lambda v: pl.BlockSpec(v.shape, lambda i, m: (0,) * v.ndim)
    chosen = [tables[s] for s in which]
    return pl.pallas_call(
        functools.partial(kernel, which),
        grid_spec=pltpu.PrefetchScalarGridSpec(
            num_scalar_prefetch=1,
            grid=(len(which),),
            in_specs=[row_spec, *map(whole, chosen), *map(whole, extra)],
            out_specs=out_specs,
        ),
        out_shape=outs,
        compiler_params=pltpu.CompilerParams(vmem_limit_bytes=40 << 20),
        cost_estimate=pl.CostEstimate(
            flops=len(which) * flops * COLS * CB * D,
            bytes_accessed=len(which) * COLS * D * 2,
            transcendentals=len(which) * COLS * CB,
        ),
        name=name,
    )(me, rows, *chosen, *extra)


def score_kernel(which, me, rows, *refs):
    tables, previous, out = refs[: len(which)], refs[len(which) : -1], refs[-1]

    @pl.when(pl.program_id(0) == 0)
    def _():
        out[...] = previous[0][...] if previous else jnp.zeros_like(out)

    def body(k):
        label = label_of(me[0], which[k])
        scores = scores_of(tables[k], rows[...].reshape(COLS, D), norms_of(tables[k]))
        highest = jnp.max(scores, axis=0, keepdims=True)
        partial = highest + jnp.log2(jnp.sum(jnp.exp2(scores - highest), axis=0, keepdims=True))
        partial = partial * LN2
        tiles = [jnp.broadcast_to(partial[:, c : c + LANES], (COPIES, LANES)) for c in range(0, COLS, LANES)]
        lanes = iota((PEERS, LANES), 1) // (CAP * PB)
        out[...] = jnp.where(lanes == label, turned_by(jnp.concatenate(tiles, axis=0), label, -1), out[...])

    each_label(which, body)


def score(me, rows, tables, which, previous):
    return call_by_label(
        score_kernel, me, rows, tables, which, previous,
        jax.ShapeDtypeStruct((PEERS, LANES), F32),
        pl.BlockSpec((PEERS, LANES), lambda i, m: (0, 0)),
        2, "score_blocks",
    )


def home_kernel(returned, peer_col, slot_col, peer_row, lse, outward):
    pick = (iota((ENTRIES, PEERS), 1) == peer_col[...]).astype(BF16)
    mask = (iota((ENTRIES, LANES), 1) // PB == slot_col[...]).astype(F32)
    mine = picked_sum(pick, returned[...]) * mask
    turn = LANES // 2
    while turn >= PB:
        mine = mine + pltpu.roll(mine, turn, 1)
        turn //= 2
    first, second = mine[:PBD], mine[PBD:]
    highest = jnp.maximum(first, second)
    total = highest + jnp.log(jnp.exp(first - highest) + jnp.exp(second - highest))
    lse[...] = total
    place = (iota((PEERS, ENTRIES), 0) == peer_row[...]).astype(BF16)
    filled = jnp.dot(place, mask.astype(BF16), preferred_element_type=F32)
    both = jnp.concatenate([total, total], axis=0)
    outward[...] = jnp.where(filled > 0.5, picked_sum(place, both * mask), EMPTY)


def home(returned, peer_col, slot_col, peer_row):
    return pl.pallas_call(
        home_kernel,
        out_shape=(
            jax.ShapeDtypeStruct((PBD, LANES), F32),
            jax.ShapeDtypeStruct((PEERS, LANES), F32),
        ),
        name="join_halves",
    )(returned, peer_col, slot_col, peer_row)


def weigh_kernel(which, me, rows, *refs):
    tables, inward, outs = refs[: len(which)], refs[len(which)], refs[len(which) + 1 :]
    mine = iota((PEERS, LANES), 1) // (CAP * PB) == iota((PEERS, LANES), 0) % COPIES

    def body(k):
        label = label_of(me[0], which[k])
        block = rows[...].reshape(COLS, D)
        turned = jnp.where(mine, turned_by(inward[...] * LOG2E, -label, 1), 0.0)
        tiles = [jnp.sum(turned[c : c + COPIES], axis=0, keepdims=True) for c in range(0, PEERS, COPIES)]
        point_lse = jnp.concatenate(tiles, axis=1)
        weights = jnp.exp2(scores_of(tables[k], block, norms_of(tables[k])) - point_lse)
        sums = jnp.dot(weights.astype(BF16), block, preferred_element_type=F32)
        mass = weights[:, :128]
        for c in range(128, COLS, 128):
            mass += weights[:, c : c + 128]
        mass = jnp.sum(mass.T, axis=0, keepdims=True)
        if which[k] == COPIES - 1:
            outs[0][...] = sums
            outs[1][...] = jnp.broadcast_to(mass, outs[1].shape)
        else:
            outs[0][0, :CB] = sums.astype(BF16)
            coarse = mass.astype(BF16)
            fine = (mass - coarse.astype(F32)).astype(BF16)
            pair = jnp.concatenate([coarse.astype(F32), fine.astype(F32)], axis=1)
            outs[0][0, CB:] = jnp.broadcast_to(pair, (MSG - CB, D)).astype(BF16)

    each_label(which, body)


def weigh(me, rows, tables, which, inward):
    if which[0] == COPIES - 1:
        outs = (jax.ShapeDtypeStruct((CB, D), F32), jax.ShapeDtypeStruct((8, CB), F32))
        specs = [pl.BlockSpec(o.shape, lambda i, m: (0, 0)) for o in outs]
    else:
        outs = (jax.ShapeDtypeStruct((len(which), MSG, D), BF16),)
        specs = [pl.BlockSpec((1, MSG, D), lambda i, m: (i, 0, 0))]
    return call_by_label(weigh_kernel, me, rows, tables, which, (inward,), outs, specs, 4, "weigh_points")


def finish_kernel(own_sum, own_mass, m0, m1, m2, table, out):
    total, mass = own_sum[...], own_mass[:1]
    for message in (m0, m1, m2):
        total += message[:CB].astype(F32)
        pair = message[CB:].astype(F32)[:1]
        mass += pair[:, :CB] + pair[:, CB:]
    column = jnp.broadcast_to(mass + 1.0, (128, CB)).T[:, :1]
    fresh = ((total + table[...].astype(F32)) / column).astype(BF16)
    out[...] = jnp.broadcast_to(fresh, out.shape)


def finish(own_sum, own_mass, arrived, table, copies):
    return pl.pallas_call(
        finish_kernel,
        out_shape=jax.ShapeDtypeStruct((*copies, CB, D), BF16),
        compiler_params=pltpu.CompilerParams(vmem_limit_bytes=16 << 20),
        name="new_centres",
    )(own_sum, own_mass, *arrived, table)


def shifted(value, by):
    return lax.ppermute(value, "zh", [(i, (i + by) % COPIES) for i in range(COPIES)])


def tables_of(own):
    return [shifted(own, COPIES - 1 - s) for s in range(COPIES - 1)] + [own]


def exchange(value):
    return lax.all_to_all(value, GROUP, split_axis=0, concat_axis=0, tiled=True)


def route(candidates):
    picked = candidates.T.reshape(-1)
    labels = jnp.arange(NCB, dtype=jnp.int32)
    member = (picked[:, None] == labels[None, :]).astype(BF16)
    index = jnp.arange(ENTRIES, dtype=jnp.int32)
    earlier = (index[None, :] < index[:, None]).astype(BF16)
    hits = jnp.dot(earlier, member, preferred_element_type=F32)
    arrival = jnp.sum(hits * member.astype(F32), axis=1).astype(jnp.int32)
    peer = picked % PEERS
    slot = picked // PEERS * CAP + arrival
    position = peer * (COPIES * CAP) + slot
    places = jnp.arange(SLOTS, dtype=jnp.int32)
    source = jnp.sum(jnp.where(position[:, None] == places[None, :], index[:, None] % PBD + 1, 0), axis=0) - 1
    return source, peer, slot


def on_device(points, centroids, candidates):
    me = lax.axis_index("zh").reshape(1)
    own = lax.dynamic_slice_in_dim(centroids, lax.axis_index("x") * CB, CB, 0)
    source, peer, slot = route(candidates)
    outgoing = pack(source, points.reshape(PBD, PB, D))
    outgoing, *tables = lax.optimization_barrier((outgoing, *tables_of(own)))
    rows = exchange(outgoing.reshape(PEERS, LANES, D))
    for iteration in range(ITERS):
        partial = score(me, rows, tables, (3,), ())
        returned = exchange(score(me, rows, tables, (0, 1, 2), (partial,)))
        lse, outward = home(returned, peer[:, None], slot[:, None], peer[None, :])
        inward = exchange(outward)
        far, inward = lax.optimization_barrier((*weigh(me, rows, tables, (1,), inward), inward))
        arrived = [shifted(far[0], 2)]
        near, inward = lax.optimization_barrier((*weigh(me, rows, tables, (0, 2), inward), inward))
        arrived += [shifted(near[0], 1), shifted(near[1], 3)]
        own_sum, own_mass = weigh(me, rows, tables, (3,), inward)
        last = iteration == ITERS - 1
        own = finish(own_sum, own_mass, arrived, own, (COPIES,) if last else ())
        if not last:
            tables = tables_of(own)
    gathered = lax.all_to_all(own, "x", split_axis=0, concat_axis=0, tiled=True)
    return gathered.reshape(COPIES * CB, D), lse[:, :PB].reshape(-1)


def solution(mesh):
    split = Mesh(mesh.devices.reshape(4, 2, 4, 2, 4), ("zh", "zl", "y", "core", "x"))
    pts = ("zh", "zl", "y", "core")
    return jax.shard_map(
        on_device,
        mesh=split,
        in_specs=(P((*pts, "x"), None), P(pts, None), P((*pts, "x"), None)),
        out_specs=(P(pts, None), P((*pts, "x"))),
        check_vma=False,
    )
```

```python
import functools
import math

import jax
import jax.numpy as jnp
from jax import lax
from jax.experimental import pallas as pl
from jax.experimental.pallas import tpu as pltpu
from jax.sharding import Mesh, PartitionSpec as P

D = 512
CB = 256
PB = 16
PBD = 128
NCB = 256
ITERS = 2
CAP = 2
COPIES = 4
PEERS = NCB // COPIES
LANES = COPIES * CAP * PB
SLOTS = PEERS * COPIES * CAP
ENTRIES = 2 * PBD
COLS = PEERS * CAP * PB
MSG = CB + 16
ORDER = (2, 1, 3)
LIMIT = 28
EMPTY = 1e30
GROUP = ("zl", "y", "core", "x")
BETA = 1.0 / math.sqrt(D)
LOG2E = 1.0 / math.log(2.0)
LN2 = math.log(2.0)
F32 = jnp.float32
BF16 = jnp.bfloat16


def picked_sum(chosen, values):
    total = None
    for _ in range(3):
        piece = values.astype(BF16)
        part = jnp.dot(chosen, piece, preferred_element_type=F32)
        total = part if total is None else total + part
        values = values - piece.astype(F32)
    return total


def iota(shape, dim):
    return lax.broadcasted_iota(jnp.int32, shape, dim)


def pack_kernel(src, points, out):
    base = pl.program_id(0) * out.shape[0]

    def body(i, carry):
        s = src[base + i]
        block = points[jnp.maximum(s, 0)]
        out[i] = jnp.where(s >= 0, block, jnp.zeros_like(block))
        return carry

    lax.fori_loop(0, out.shape[0], body, 0, unroll=8)


def pack(src, points):
    per = 128
    return pl.pallas_call(
        pack_kernel,
        grid_spec=pltpu.PrefetchScalarGridSpec(
            num_scalar_prefetch=1,
            grid=(SLOTS // per,),
            in_specs=[pl.BlockSpec((PBD, PB, D), lambda i, s: (0, 0, 0))],
            out_specs=pl.BlockSpec((per, PB, D), lambda i, s: (i, 0, 0)),
        ),
        out_shape=jax.ShapeDtypeStruct((SLOTS, PB, D), BF16),
        compiler_params=pltpu.CompilerParams(vmem_limit_bytes=20 << 20),
        name="pack_points",
    )(src, points)


def norms_of(table):
    wide = table[...].astype(F32)
    return (BETA * LOG2E) * jnp.sum(wide * wide, axis=1, keepdims=True)


def scores_of(table, block, norms):
    products = lax.dot_general(table[...], block, (((1,), (1,)), ((), ())), preferred_element_type=F32)
    return (2.0 * BETA * LOG2E) * products - norms


def turned_by(value, groups, per_row):
    row = iota(value.shape, 0) % COPIES
    turned = value
    for k in range(COPIES):
        turn = lax.rem(groups + per_row * k + 2 * COPIES, COPIES) * (CAP * PB)
        turned = jnp.where(row == k, pltpu.roll(value, turn, 1), turned)
    return turned


def label_of(me, s):
    return lax.rem(me + 1 + s, COPIES)


def call_whole(kernel, me, rows, tables, which, extra, outs, flops, name):
    return pl.pallas_call(
        functools.partial(kernel, which),
        in_specs=[pl.BlockSpec(memory_space=pltpu.SMEM)]
        + [pl.BlockSpec(memory_space=pltpu.VMEM)] * (1 + len(which) + len(extra)),
        out_shape=outs,
        compiler_params=pltpu.CompilerParams(vmem_limit_bytes=LIMIT << 20),
        cost_estimate=pl.CostEstimate(
            flops=len(which) * flops * COLS * CB * D,
            bytes_accessed=len(which) * COLS * D * 2,
            transcendentals=len(which) * COLS * CB,
        ),
        name=name,
    )(me, rows, *[tables[s] for s in which], *extra)


def keep_kernel(source, kept, done):
    copy = pltpu.make_async_copy(source, kept, done)
    copy.start()
    copy.wait()


def keep(rows):
    return pl.pallas_call(
        keep_kernel,
        in_specs=[pl.BlockSpec(memory_space=pl.ANY)],
        out_specs=pl.BlockSpec(memory_space=pltpu.VMEM),
        out_shape=jax.ShapeDtypeStruct(rows.shape, rows.dtype),
        scratch_shapes=[pltpu.SemaphoreType.DMA],
        compiler_params=pltpu.CompilerParams(vmem_limit_bytes=LIMIT << 20),
        name="keep_points",
    )(rows)


def rows_of(rows, label):
    part = rows[:, pl.ds(pl.multiple_of(label * (CAP * PB), CAP * PB), CAP * PB), :]
    return part.reshape(COLS, D)


def score_kernel(which, me, rows, *refs):
    tables, out = refs[:-1], refs[-1]
    lanes = iota((PEERS, LANES), 1) // (CAP * PB)
    total = jnp.zeros((PEERS, LANES), F32)
    for k, s in enumerate(which):
        label = label_of(me[0], s)
        scores = scores_of(tables[k], rows_of(rows, label), norms_of(tables[k]))
        highest = jnp.max(scores, axis=0, keepdims=True)
        partial = highest + jnp.log2(jnp.sum(jnp.exp2(scores - highest), axis=0, keepdims=True))
        partial = partial * LN2
        tiles = [jnp.broadcast_to(partial[:, c : c + LANES], (COPIES, LANES)) for c in range(0, COLS, LANES)]
        total = jnp.where(lanes == label, turned_by(jnp.concatenate(tiles, axis=0), label, -1), total)
    out[...] = total


def score(me, rows, tables):
    out = jax.ShapeDtypeStruct((PEERS, LANES), F32)
    return call_whole(score_kernel, me, rows, tables, (0, 1, 2, 3), (), out, 2, "score_blocks")


def home_kernel(returned, peer_col, slot_col, peer_row, lse, outward):
    pick = (iota((ENTRIES, PEERS), 1) == peer_col[...]).astype(BF16)
    mask = (iota((ENTRIES, LANES), 1) // PB == slot_col[...]).astype(F32)
    mine = picked_sum(pick, returned[...]) * mask
    turn = LANES // 2
    while turn >= PB:
        mine = mine + pltpu.roll(mine, turn, 1)
        turn //= 2
    first, second = mine[:PBD], mine[PBD:]
    highest = jnp.maximum(first, second)
    total = highest + jnp.log(jnp.exp(first - highest) + jnp.exp(second - highest))
    lse[...] = total
    place = (iota((PEERS, ENTRIES), 0) == peer_row[...]).astype(BF16)
    filled = jnp.dot(place, mask.astype(BF16), preferred_element_type=F32)
    both = jnp.concatenate([total, total], axis=0)
    outward[...] = jnp.where(filled > 0.5, picked_sum(place, both * mask), EMPTY)


def home(returned, peer_col, slot_col, peer_row):
    return pl.pallas_call(
        home_kernel,
        out_shape=(
            jax.ShapeDtypeStruct((PBD, LANES), F32),
            jax.ShapeDtypeStruct((PEERS, LANES), F32),
        ),
        compiler_params=pltpu.CompilerParams(vmem_limit_bytes=8 << 20),
        name="join_halves",
    )(returned, peer_col, slot_col, peer_row)


def weigh_kernel(which, me, rows, *refs):
    tables, inward, outs = refs[: len(which)], refs[len(which)], refs[len(which) + 1 :]
    mine = iota((PEERS, LANES), 1) // (CAP * PB) == iota((PEERS, LANES), 0) % COPIES
    incoming = inward[...] * LOG2E
    for k, s in enumerate(which):
        label = label_of(me[0], s)
        block = rows_of(rows, label)
        turned = jnp.where(mine, turned_by(incoming, -label, 1), 0.0)
        tiles = [jnp.sum(turned[c : c + COPIES], axis=0, keepdims=True) for c in range(0, PEERS, COPIES)]
        point_lse = jnp.concatenate(tiles, axis=1)
        weights = jnp.exp2(scores_of(tables[k], block, norms_of(tables[k])) - point_lse)
        sums = jnp.dot(weights.astype(BF16), block, preferred_element_type=F32)
        mass = weights[:, :128]
        for c in range(128, COLS, 128):
            mass += weights[:, c : c + 128]
        mass = jnp.sum(mass.T, axis=0, keepdims=True)
        if s == COPIES - 1:
            outs[0][...] = sums
            outs[1][...] = jnp.broadcast_to(mass, outs[1].shape)
            continue
        coarse = mass.astype(BF16).astype(F32)
        fine = mass - coarse
        outs[0][k, :CB] = sums.astype(BF16)
        pair = jnp.concatenate([coarse, fine], axis=1)
        outs[0][k, CB:] = jnp.broadcast_to(pair, (MSG - CB, D)).astype(BF16)


def weigh_own(me, rows, tables, inward):
    outs = (jax.ShapeDtypeStruct((CB, D), F32), jax.ShapeDtypeStruct((8, CB), F32))
    return call_whole(weigh_kernel, me, rows, tables, (3,), (inward,), outs, 4, "weigh_own")


def weigh_others(me, rows, tables, inward):
    out = jax.ShapeDtypeStruct((COPIES - 1, MSG, D), BF16)
    return call_whole(weigh_kernel, me, rows, tables, (0, 1, 2), (inward,), out, 4, "weigh_others")


def finish_kernel(own_sum, own_mass, m0, m1, m2, table, out):
    total, mass = own_sum[...], own_mass[:1]
    for message in (m0, m1, m2):
        total += message[:CB].astype(F32)
        pair = message[CB:].astype(F32)[:1]
        mass += pair[:, :CB] + pair[:, CB:]
    column = jnp.broadcast_to(mass + 1.0, (128, CB)).T[:, :1]
    fresh = ((total + table[...].astype(F32)) / column).astype(BF16)
    out[...] = jnp.broadcast_to(fresh, out.shape)


def finish(own_sum, own_mass, arrived, table, copies):
    return pl.pallas_call(
        finish_kernel,
        out_shape=jax.ShapeDtypeStruct((*copies, CB, D), BF16),
        compiler_params=pltpu.CompilerParams(vmem_limit_bytes=16 << 20),
        name="new_centres",
    )(own_sum, own_mass, *arrived, table)


def shifted(value, by):
    return lax.ppermute(value, "zh", [(i, (i + by) % COPIES) for i in range(COPIES)])


def tables_of(own):
    return [shifted(own, COPIES - 1 - s) for s in range(COPIES - 1)] + [own]


def exchange(value):
    return lax.all_to_all(value, GROUP, split_axis=0, concat_axis=0, tiled=True)


def route(candidates):
    picked = candidates.T.reshape(-1)
    labels = jnp.arange(NCB, dtype=jnp.int32)
    member = (picked[:, None] == labels[None, :]).astype(BF16)
    index = jnp.arange(ENTRIES, dtype=jnp.int32)
    earlier = (index[None, :] < index[:, None]).astype(BF16)
    hits = jnp.dot(earlier, member, preferred_element_type=F32)
    arrival = jnp.sum(hits * member.astype(F32), axis=1).astype(jnp.int32)
    peer = picked % PEERS
    slot = picked // PEERS * CAP + arrival
    position = peer * (COPIES * CAP) + slot
    places = jnp.arange(SLOTS, dtype=jnp.int32)
    source = jnp.sum(jnp.where(position[:, None] == places[None, :], index[:, None] % PBD + 1, 0), axis=0) - 1
    return source, peer, slot


def on_device(points, centroids, candidates):
    me = lax.axis_index("zh").reshape(1)
    own = lax.dynamic_slice_in_dim(centroids, lax.axis_index("x") * CB, CB, 0)
    source, peer, slot = route(candidates)
    outgoing = pack(source, points.reshape(PBD, PB, D))
    where = (peer[:, None], slot[:, None], peer[None, :])
    outgoing, where, tables = lax.optimization_barrier((outgoing, where, tables_of(own)))
    rows = keep(exchange(outgoing.reshape(PEERS, LANES, D)))
    for iteration in range(ITERS):
        returned = exchange(score(me, rows, tables))
        lse, outward = home(returned, *where)
        inward = exchange(outward)
        last = iteration == ITERS - 1
        messages = weigh_others(me, rows, tables, inward)
        arrived = [shifted(messages[n - 1], n) for n in ORDER]
        messages, inward = lax.optimization_barrier((messages, inward))
        own_sum, own_mass = weigh_own(me, rows, tables, inward)
        own = finish(own_sum, own_mass, arrived, own, (COPIES,) if last else ())
        if not last:
            tables = tables_of(own)
    gathered = lax.all_to_all(own, "x", split_axis=0, concat_axis=0, tiled=True)
    return gathered.reshape(COPIES * CB, D), lse[:, :PB].reshape(-1)


def solution(mesh):
    split = Mesh(mesh.devices.reshape(4, 2, 4, 2, 4), ("zh", "zl", "y", "core", "x"))
    pts = ("zh", "zl", "y", "core")
    return jax.shard_map(
        on_device,
        mesh=split,
        in_specs=(P((*pts, "x"), None), P(pts, None), P((*pts, "x"), None)),
        out_specs=(P(pts, None), P((*pts, "x"))),
        check_vma=False,
    )
```

```python
import functools
import math

import jax
import jax.numpy as jnp
from jax import lax
from jax.experimental import pallas as pl
from jax.experimental.pallas import tpu as pltpu
from jax.sharding import Mesh, PartitionSpec as P

D = 512
CB = 256
PB = 16
PBD = 128
NCB = 256
ITERS = 2
CAP = 2
COPIES = 4
PEERS = NCB // COPIES
LANES = COPIES * CAP * PB
SLOTS = PEERS * COPIES * CAP
ENTRIES = 2 * PBD
COLS = PEERS * CAP * PB
MSG = CB + 16
ORDER = (2, 1, 3)
LIMIT = 28
EMPTY = 1e30
GROUP = ("zl", "y", "core", "x")
BETA = 1.0 / math.sqrt(D)
LOG2E = 1.0 / math.log(2.0)
LN2 = math.log(2.0)
F32 = jnp.float32
BF16 = jnp.bfloat16


def picked_sum(chosen, values):
    total = None
    for _ in range(3):
        piece = values.astype(BF16)
        part = jnp.dot(chosen, piece, preferred_element_type=F32)
        total = part if total is None else total + part
        values = values - piece.astype(F32)
    return total


def iota(shape, dim):
    return lax.broadcasted_iota(jnp.int32, shape, dim)


def pack_kernel(src, points, out):
    base = pl.program_id(0) * out.shape[0]

    def body(i, carry):
        s = src[base + i]
        block = points[jnp.maximum(s, 0)]
        out[i] = jnp.where(s >= 0, block, jnp.zeros_like(block))
        return carry

    lax.fori_loop(0, out.shape[0], body, 0, unroll=8)


def pack(src, points):
    per = 128
    return pl.pallas_call(
        pack_kernel,
        grid_spec=pltpu.PrefetchScalarGridSpec(
            num_scalar_prefetch=1,
            grid=(SLOTS // per,),
            in_specs=[pl.BlockSpec((PBD, PB, D), lambda i, s: (0, 0, 0))],
            out_specs=pl.BlockSpec((per, PB, D), lambda i, s: (i, 0, 0)),
        ),
        out_shape=jax.ShapeDtypeStruct((SLOTS, PB, D), BF16),
        compiler_params=pltpu.CompilerParams(vmem_limit_bytes=58 << 20),
        name="pack_points",
    )(src, points)


def norms_of(table):
    wide = table[...].astype(F32)
    return (BETA * LOG2E) * jnp.sum(wide * wide, axis=1, keepdims=True)


def scores_of(table, block, norms):
    products = lax.dot_general(table[...], block, (((1,), (1,)), ((), ())), preferred_element_type=F32)
    return (2.0 * BETA * LOG2E) * products - norms


def turned_by(value, groups, per_row):
    row = iota(value.shape, 0) % COPIES
    turned = value
    for k in range(COPIES):
        turn = lax.rem(groups + per_row * k + 2 * COPIES, COPIES) * (CAP * PB)
        turned = jnp.where(row == k, pltpu.roll(value, turn, 1), turned)
    return turned


def label_of(me, s):
    return lax.rem(me + 1 + s, COPIES)


def call_whole(kernel, me, rows, tables, which, extra, outs, flops, name):
    return pl.pallas_call(
        functools.partial(kernel, which),
        in_specs=[pl.BlockSpec(memory_space=pltpu.SMEM)]
        + [pl.BlockSpec(memory_space=pltpu.VMEM)] * (1 + len(which) + len(extra)),
        out_shape=outs,
        compiler_params=pltpu.CompilerParams(vmem_limit_bytes=LIMIT << 20),
        cost_estimate=pl.CostEstimate(
            flops=len(which) * flops * COLS * CB * D,
            bytes_accessed=len(which) * COLS * D * 2,
            transcendentals=len(which) * COLS * CB,
        ),
        name=name,
    )(me, rows, *[tables[s] for s in which], *extra)


def keep_kernel(source, kept, done):
    copy = pltpu.make_async_copy(source, kept, done)
    copy.start()
    copy.wait()


def keep(rows):
    return pl.pallas_call(
        keep_kernel,
        in_specs=[pl.BlockSpec(memory_space=pl.ANY)],
        out_specs=pl.BlockSpec(memory_space=pltpu.VMEM),
        out_shape=jax.ShapeDtypeStruct(rows.shape, rows.dtype),
        scratch_shapes=[pltpu.SemaphoreType.DMA],
        compiler_params=pltpu.CompilerParams(vmem_limit_bytes=LIMIT << 20),
        name="keep_points",
    )(rows)


def rows_of(rows, label):
    part = rows[:, pl.ds(pl.multiple_of(label * (CAP * PB), CAP * PB), CAP * PB), :]
    return part.reshape(COLS, D)


def score_kernel(which, me, rows, *refs):
    tables, previous, out = refs[: len(which)], refs[len(which) : -1], refs[-1]
    lanes = iota((PEERS, LANES), 1) // (CAP * PB)
    total = previous[0][...] if previous else jnp.zeros((PEERS, LANES), F32)
    for k, s in enumerate(which):
        label = label_of(me[0], s)
        scores = scores_of(tables[k], rows_of(rows, label), norms_of(tables[k]))
        highest = jnp.max(scores, axis=0, keepdims=True)
        partial = highest + jnp.log2(jnp.sum(jnp.exp2(scores - highest), axis=0, keepdims=True))
        partial = partial * LN2
        tiles = [jnp.broadcast_to(partial[:, c : c + LANES], (COPIES, LANES)) for c in range(0, COLS, LANES)]
        total = jnp.where(lanes == label, turned_by(jnp.concatenate(tiles, axis=0), label, -1), total)
    out[...] = total


def score(me, rows, tables):
    out = jax.ShapeDtypeStruct((PEERS, LANES), F32)
    partial = call_whole(score_kernel, me, rows, tables, (0, 2, 3), (), out, 2, "score_near")
    return call_whole(score_kernel, me, rows, tables, (1,), (partial,), out, 2, "score_far")


def home_kernel(returned, peer_col, slot_col, peer_row, lse, outward):
    pick = (iota((ENTRIES, PEERS), 1) == peer_col[...]).astype(BF16)
    mask = (iota((ENTRIES, LANES), 1) // PB == slot_col[...]).astype(F32)
    mine = picked_sum(pick, returned[...]) * mask
    turn = LANES // 2
    while turn >= PB:
        mine = mine + pltpu.roll(mine, turn, 1)
        turn //= 2
    first, second = mine[:PBD], mine[PBD:]
    highest = jnp.maximum(first, second)
    total = highest + jnp.log(jnp.exp(first - highest) + jnp.exp(second - highest))
    lse[...] = total
    place = (iota((PEERS, ENTRIES), 0) == peer_row[...]).astype(BF16)
    filled = jnp.dot(place, mask.astype(BF16), preferred_element_type=F32)
    both = jnp.concatenate([total, total], axis=0)
    outward[...] = jnp.where(filled > 0.5, picked_sum(place, both * mask), EMPTY)


def home(returned, peer_col, slot_col, peer_row):
    return pl.pallas_call(
        home_kernel,
        out_shape=(
            jax.ShapeDtypeStruct((PBD, LANES), F32),
            jax.ShapeDtypeStruct((PEERS, LANES), F32),
        ),
        compiler_params=pltpu.CompilerParams(vmem_limit_bytes=8 << 20),
        name="join_halves",
    )(returned, peer_col, slot_col, peer_row)


def weigh_kernel(which, me, rows, *refs):
    tables, inward, outs = refs[: len(which)], refs[len(which)], refs[len(which) + 1 :]
    mine = iota((PEERS, LANES), 1) // (CAP * PB) == iota((PEERS, LANES), 0) % COPIES
    incoming = inward[...] * LOG2E
    for k, s in enumerate(which):
        label = label_of(me[0], s)
        block = rows_of(rows, label)
        turned = jnp.where(mine, turned_by(incoming, -label, 1), 0.0)
        tiles = [jnp.sum(turned[c : c + COPIES], axis=0, keepdims=True) for c in range(0, PEERS, COPIES)]
        point_lse = jnp.concatenate(tiles, axis=1)
        weights = jnp.exp2(scores_of(tables[k], block, norms_of(tables[k])) - point_lse)
        sums = jnp.dot(weights.astype(BF16), block, preferred_element_type=F32)
        mass = weights[:, :128]
        for c in range(128, COLS, 128):
            mass += weights[:, c : c + 128]
        mass = jnp.sum(mass.T, axis=0, keepdims=True)
        if s == COPIES - 1:
            outs[0][...] = sums
            outs[1][...] = jnp.broadcast_to(mass, outs[1].shape)
            continue
        coarse = mass.astype(BF16).astype(F32)
        fine = mass - coarse
        outs[0][k, :CB] = sums.astype(BF16)
        pair = jnp.concatenate([coarse, fine], axis=1)
        outs[0][k, CB:] = jnp.broadcast_to(pair, (MSG - CB, D)).astype(BF16)


def weigh_own(me, rows, tables, inward):
    outs = (jax.ShapeDtypeStruct((CB, D), F32), jax.ShapeDtypeStruct((8, CB), F32))
    return call_whole(weigh_kernel, me, rows, tables, (3,), (inward,), outs, 4, "weigh_own")


def weigh_others(me, rows, tables, inward):
    out = jax.ShapeDtypeStruct((COPIES - 1, MSG, D), BF16)
    return call_whole(weigh_kernel, me, rows, tables, (0, 1, 2), (inward,), out, 4, "weigh_others")


def finish_kernel(own_sum, own_mass, m0, m1, m2, table, out):
    total, mass = own_sum[...], own_mass[:1]
    for message in (m0, m1, m2):
        total += message[:CB].astype(F32)
        pair = message[CB:].astype(F32)[:1]
        mass += pair[:, :CB] + pair[:, CB:]
    column = jnp.broadcast_to(mass + 1.0, (128, CB)).T[:, :1]
    fresh = ((total + table[...].astype(F32)) / column).astype(BF16)
    out[...] = jnp.broadcast_to(fresh, out.shape)


def finish(own_sum, own_mass, arrived, table, copies):
    return pl.pallas_call(
        finish_kernel,
        out_shape=jax.ShapeDtypeStruct((*copies, CB, D), BF16),
        compiler_params=pltpu.CompilerParams(vmem_limit_bytes=16 << 20),
        name="new_centres",
    )(own_sum, own_mass, *arrived, table)


def shifted(value, by):
    return lax.ppermute(value, "zh", [(i, (i + by) % COPIES) for i in range(COPIES)])


def tables_of(own):
    return [shifted(own, COPIES - 1 - s) for s in range(COPIES - 1)] + [own]


def exchange(value):
    return lax.all_to_all(value, GROUP, split_axis=0, concat_axis=0, tiled=True)


def route(candidates):
    picked = candidates.T.reshape(-1)
    labels = jnp.arange(NCB, dtype=jnp.int32)
    member = (picked[:, None] == labels[None, :]).astype(BF16)
    index = jnp.arange(ENTRIES, dtype=jnp.int32)
    earlier = (index[None, :] < index[:, None]).astype(BF16)
    hits = jnp.dot(earlier, member, preferred_element_type=F32)
    arrival = jnp.sum(hits * member.astype(F32), axis=1).astype(jnp.int32)
    peer = picked % PEERS
    slot = picked // PEERS * CAP + arrival
    position = peer * (COPIES * CAP) + slot
    places = jnp.arange(SLOTS, dtype=jnp.int32)
    source = jnp.sum(jnp.where(position[:, None] == places[None, :], index[:, None] % PBD + 1, 0), axis=0) - 1
    return source, peer, slot


def on_device(points, centroids, candidates):
    me = lax.axis_index("zh").reshape(1)
    own = lax.dynamic_slice_in_dim(centroids, lax.axis_index("x") * CB, CB, 0)
    source, peer, slot = route(candidates)
    outgoing = pack(source, points.reshape(PBD, PB, D))
    where = (peer[:, None], slot[:, None], peer[None, :])
    tables = tables_of(own)
    outgoing, tables[0], tables[2] = lax.optimization_barrier((outgoing, tables[0], tables[2]))
    rows, where = lax.optimization_barrier((exchange(outgoing.reshape(PEERS, LANES, D)), where))
    rows = keep(rows)
    for iteration in range(ITERS):
        returned = exchange(score(me, rows, tables))
        lse, outward = home(returned, *where)
        inward = exchange(outward)
        last = iteration == ITERS - 1
        messages = weigh_others(me, rows, tables, inward)
        arrived = [shifted(messages[n - 1], n) for n in ORDER]
        messages, inward = lax.optimization_barrier((messages, inward))
        own_sum, own_mass = weigh_own(me, rows, tables, inward)
        own = finish(own_sum, own_mass, arrived, own, (COPIES,) if last else ())
        if not last:
            tables = tables_of(own)
    gathered = lax.all_to_all(own, "x", split_axis=0, concat_axis=0, tiled=True)
    return gathered.reshape(COPIES * CB, D), lse[:, :PB].reshape(-1)


def solution(mesh):
    split = Mesh(mesh.devices.reshape(4, 2, 4, 2, 4), ("zh", "zl", "y", "core", "x"))
    pts = ("zh", "zl", "y", "core")
    return jax.shard_map(
        on_device,
        mesh=split,
        in_specs=(P((*pts, "x"), None), P(pts, None), P((*pts, "x"), None)),
        out_specs=(P(pts, None), P((*pts, "x"))),
        check_vma=False,
    )
```

```python
import functools
import math

import jax
import jax.numpy as jnp
from jax import lax
from jax.experimental import pallas as pl
from jax.experimental.pallas import tpu as pltpu
from jax.sharding import Mesh, PartitionSpec as P

D = 512
CB = 256
PB = 16
PBD = 128
NCB = 256
ITERS = 2
CAP = 2
COPIES = 4
PEERS = NCB // COPIES
LANES = COPIES * CAP * PB
SLOTS = PEERS * COPIES * CAP
ENTRIES = 2 * PBD
COLS = PEERS * CAP * PB
MSG = CB + 16
LIMIT = 28
QUARTERS = 4
EMPTY = 1e30
GROUP = ("zl", "y", "core", "x")
BETA = 1.0 / math.sqrt(D)
LOG2E = 1.0 / math.log(2.0)
LN2 = math.log(2.0)
F32 = jnp.float32
BF16 = jnp.bfloat16


def picked_sum(chosen, values):
    total = None
    for _ in range(3):
        piece = values.astype(BF16)
        part = jnp.dot(chosen, piece, preferred_element_type=F32)
        total = part if total is None else total + part
        values = values - piece.astype(F32)
    return total


def iota(shape, dim):
    return lax.broadcasted_iota(jnp.int32, shape, dim)


def pack_kernel(src, points, out):
    base = pl.program_id(0) * out.shape[0]

    def body(i, carry):
        s = src[base + i]
        block = points[jnp.maximum(s, 0)]
        out[i] = jnp.where(s >= 0, block, jnp.zeros_like(block))
        return carry

    lax.fori_loop(0, out.shape[0], body, 0, unroll=8)


def pack(src, points):
    per = 128
    return pl.pallas_call(
        pack_kernel,
        grid_spec=pltpu.PrefetchScalarGridSpec(
            num_scalar_prefetch=1,
            grid=(SLOTS // per,),
            in_specs=[pl.BlockSpec((PBD, PB, D), lambda i, s: (0, 0, 0))],
            out_specs=pl.BlockSpec((per, PB, D), lambda i, s: (i, 0, 0)),
        ),
        out_shape=jax.ShapeDtypeStruct((SLOTS, PB, D), BF16),
        compiler_params=pltpu.CompilerParams(vmem_limit_bytes=58 << 20),
        name="pack_points",
    )(src, points)


def norms_of(table):
    wide = table[...].astype(F32)
    return (BETA * LOG2E) * jnp.sum(wide * wide, axis=1, keepdims=True)


def scores_of(table, block, norms):
    products = lax.dot_general(table[...], block, (((1,), (1,)), ((), ())), preferred_element_type=F32)
    return (2.0 * BETA * LOG2E) * products - norms


def turned_by(value, groups, per_row):
    row = iota(value.shape, 0) % COPIES
    turned = value
    for k in range(COPIES):
        turn = lax.rem(groups + per_row * k + 2 * COPIES, COPIES) * (CAP * PB)
        turned = jnp.where(row == k, pltpu.roll(value, turn, 1), turned)
    return turned


def label_of(me, s):
    return lax.rem(me + 1 + s, COPIES)


def call_whole(kernel, me, rows, tables, which, extra, outs, flops, name):
    return pl.pallas_call(
        functools.partial(kernel, which),
        in_specs=[pl.BlockSpec(memory_space=pltpu.SMEM)]
        + [pl.BlockSpec(memory_space=pltpu.VMEM)] * (1 + len(which) + len(extra)),
        out_shape=outs,
        compiler_params=pltpu.CompilerParams(vmem_limit_bytes=LIMIT << 20),
        name=name,
    )(me, rows, *[tables[s] for s in which], *extra)


def rows_of(rows, label):
    part = rows[:, pl.ds(pl.multiple_of(label * (CAP * PB), CAP * PB), CAP * PB), :]
    return part.reshape(COLS, D)


def scored(total, table, norms, block, label):
    scores = scores_of(table, block, norms)
    highest = jnp.max(scores, axis=0, keepdims=True)
    partial = highest + jnp.log2(jnp.sum(jnp.exp2(scores - highest), axis=0, keepdims=True))
    partial = partial * LN2
    tiles = [jnp.broadcast_to(partial[:, c : c + LANES], (COPIES, LANES)) for c in range(0, block.shape[0], LANES)]
    lanes = iota(total.shape, 1) // (CAP * PB)
    return jnp.where(lanes == label, turned_by(jnp.concatenate(tiles, axis=0), label, -1), total)


def score_kernel(which, me, rows, *refs):
    tables, previous, out = refs[: len(which)], refs[len(which) : -1], refs[-1]
    total = previous[0][...] if previous else jnp.zeros((PEERS, LANES), F32)
    for k, s in enumerate(which):
        label = label_of(me[0], s)
        total = scored(total, tables[k], norms_of(tables[k]), rows_of(rows, label), label)
    out[...] = total


def keep_kernel(which, me, source, *refs):
    tables, (kept, out, done) = refs[: len(which)], refs[len(which) :]
    per = PEERS // QUARTERS
    parts = [pl.ds(i * per, per) for i in range(QUARTERS)]
    copies = [pltpu.make_async_copy(source.at[p], kept.at[p], done.at[i]) for i, p in enumerate(parts)]
    for copy in copies:
        copy.start()
    norms = [norms_of(table) for table in tables]
    for copy, part in zip(copies, parts):
        copy.wait()
        total = jnp.zeros((per, LANES), F32)
        for k, s in enumerate(which):
            label = label_of(me[0], s)
            width = CAP * PB
            block = kept[part, pl.ds(pl.multiple_of(label * width, width), width), :]
            total = scored(total, tables[k], norms[k], block.reshape(per * width, D), label)
        out[part, :] = total


def score_kept(me, received, tables):
    which = (0, 2, 3)
    vmem = pl.BlockSpec(memory_space=pltpu.VMEM)
    return pl.pallas_call(
        functools.partial(keep_kernel, which),
        in_specs=[pl.BlockSpec(memory_space=pltpu.SMEM), pl.BlockSpec(memory_space=pl.ANY)] + [vmem] * len(which),
        out_specs=(vmem, vmem),
        out_shape=(
            jax.ShapeDtypeStruct(received.shape, received.dtype),
            jax.ShapeDtypeStruct((PEERS, LANES), F32),
        ),
        scratch_shapes=[pltpu.SemaphoreType.DMA((QUARTERS,))],
        compiler_params=pltpu.CompilerParams(vmem_limit_bytes=LIMIT << 20),
        name="keep_and_score",
    )(me, received, *[tables[s] for s in which])


def score_near(me, rows, tables):
    out = jax.ShapeDtypeStruct((PEERS, LANES), F32)
    return call_whole(score_kernel, me, rows, tables, (0, 2, 3), (), out, 2, "score_near")


def score_far(me, rows, tables, partial):
    out = jax.ShapeDtypeStruct((PEERS, LANES), F32)
    return call_whole(score_kernel, me, rows, tables, (1,), (partial,), out, 2, "score_far")


def home_kernel(returned, peer_col, slot_col, peer_row, lse, outward):
    pick = (iota((ENTRIES, PEERS), 1) == peer_col[...]).astype(BF16)
    mask = (iota((ENTRIES, LANES), 1) // PB == slot_col[...]).astype(F32)
    mine = picked_sum(pick, returned[...]) * mask
    turn = LANES // 2
    while turn >= PB:
        mine = mine + pltpu.roll(mine, turn, 1)
        turn //= 2
    first, second = mine[:PBD], mine[PBD:]
    highest = jnp.maximum(first, second)
    total = highest + jnp.log(jnp.exp(first - highest) + jnp.exp(second - highest))
    lse[...] = total
    place = (iota((PEERS, ENTRIES), 0) == peer_row[...]).astype(BF16)
    filled = jnp.dot(place, mask.astype(BF16), preferred_element_type=F32)
    both = jnp.concatenate([total, total], axis=0)
    outward[...] = jnp.where(filled > 0.5, picked_sum(place, both * mask), EMPTY)


def home(returned, peer_col, slot_col, peer_row):
    return pl.pallas_call(
        home_kernel,
        out_shape=(
            jax.ShapeDtypeStruct((PBD, LANES), F32),
            jax.ShapeDtypeStruct((PEERS, LANES), F32),
        ),
        compiler_params=pltpu.CompilerParams(vmem_limit_bytes=8 << 20),
        name="join_halves",
    )(returned, peer_col, slot_col, peer_row)


def weigh_kernel(which, me, rows, *refs):
    tables, inward, outs = refs[: len(which)], refs[len(which)], refs[len(which) + 1 :]
    mine = iota((PEERS, LANES), 1) // (CAP * PB) == iota((PEERS, LANES), 0) % COPIES
    incoming = inward[...] * LOG2E
    for k, s in enumerate(which):
        label = label_of(me[0], s)
        block = rows_of(rows, label)
        turned = jnp.where(mine, turned_by(incoming, -label, 1), 0.0)
        tiles = [jnp.sum(turned[c : c + COPIES], axis=0, keepdims=True) for c in range(0, PEERS, COPIES)]
        point_lse = jnp.concatenate(tiles, axis=1)
        weights = jnp.exp2(scores_of(tables[k], block, norms_of(tables[k])) - point_lse)
        sums = jnp.dot(weights.astype(BF16), block, preferred_element_type=F32)
        mass = weights[:, :128]
        for c in range(128, COLS, 128):
            mass += weights[:, c : c + 128]
        mass = jnp.sum(mass.T, axis=0, keepdims=True)
        if s == COPIES - 1:
            outs[0][...] = sums
            outs[1][...] = jnp.broadcast_to(mass, outs[1].shape)
            continue
        coarse = mass.astype(BF16).astype(F32)
        fine = mass - coarse
        outs[0][k, :CB] = sums.astype(BF16)
        pair = jnp.concatenate([coarse, fine], axis=1)
        outs[0][k, CB:] = jnp.broadcast_to(pair, (MSG - CB, D)).astype(BF16)


def weigh_own(me, rows, tables, inward):
    outs = (jax.ShapeDtypeStruct((CB, D), F32), jax.ShapeDtypeStruct((8, CB), F32))
    return call_whole(weigh_kernel, me, rows, tables, (3,), (inward,), outs, 4, "weigh_own")


def weigh_others(me, rows, tables, which, inward):
    out = jax.ShapeDtypeStruct((len(which), MSG, D), BF16)
    return call_whole(weigh_kernel, me, rows, tables, which, (inward,), out, 4, "weigh_others")


def merge_kernel(own_sum, own_mass, message, total, mass):
    total[...] = own_sum[...] + message[:CB].astype(F32)
    pair = message[CB:].astype(F32)[:1]
    mass[...] = own_mass[...] + pair[:, :CB] + pair[:, CB:]


def merge(own_sum, own_mass, message):
    return pl.pallas_call(
        merge_kernel,
        out_shape=(jax.ShapeDtypeStruct((CB, D), F32), jax.ShapeDtypeStruct((8, CB), F32)),
        compiler_params=pltpu.CompilerParams(vmem_limit_bytes=16 << 20),
        name="merge_far",
    )(own_sum, own_mass, message)


def finish_kernel(own_sum, own_mass, m1, m2, table, out):
    total, mass = own_sum[...], own_mass[:1]
    for message in (m1, m2):
        total += message[:CB].astype(F32)
        pair = message[CB:].astype(F32)[:1]
        mass += pair[:, :CB] + pair[:, CB:]
    column = jnp.broadcast_to(mass + 1.0, (128, CB)).T[:, :1]
    fresh = ((total + table[...].astype(F32)) / column).astype(BF16)
    out[...] = jnp.broadcast_to(fresh, out.shape)


def finish(own_sum, own_mass, arrived, table, copies):
    return pl.pallas_call(
        finish_kernel,
        out_shape=jax.ShapeDtypeStruct((*copies, CB, D), BF16),
        compiler_params=pltpu.CompilerParams(vmem_limit_bytes=16 << 20),
        name="new_centres",
    )(own_sum, own_mass, *arrived, table)


def shifted(value, by):
    return lax.ppermute(value, "zh", [(i, (i + by) % COPIES) for i in range(COPIES)])


def tables_of(own):
    return [shifted(own, COPIES - 1 - s) for s in range(COPIES - 1)] + [own]


def exchange(value):
    return lax.all_to_all(value, GROUP, split_axis=0, concat_axis=0, tiled=True)


def route(candidates):
    picked = candidates.T.reshape(-1)
    labels = jnp.arange(NCB, dtype=jnp.int32)
    member = (picked[:, None] == labels[None, :]).astype(BF16)
    index = jnp.arange(ENTRIES, dtype=jnp.int32)
    earlier = (index[None, :] < index[:, None]).astype(BF16)
    hits = jnp.dot(earlier, member, preferred_element_type=F32)
    arrival = jnp.sum(hits * member.astype(F32), axis=1).astype(jnp.int32)
    peer = picked % PEERS
    slot = picked // PEERS * CAP + arrival
    position = peer * (COPIES * CAP) + slot
    places = jnp.arange(SLOTS, dtype=jnp.int32)
    source = jnp.sum(jnp.where(position[:, None] == places[None, :], index[:, None] % PBD + 1, 0), axis=0) - 1
    return source, peer, slot


def on_device(points, centroids, candidates):
    me = lax.axis_index("zh").reshape(1)
    own = lax.dynamic_slice_in_dim(centroids, lax.axis_index("x") * CB, CB, 0)
    source, peer, slot = route(candidates)
    outgoing = pack(source, points.reshape(PBD, PB, D))
    where = (peer[:, None], slot[:, None], peer[None, :])
    tables = tables_of(own)
    outgoing, tables[0], tables[2] = lax.optimization_barrier((outgoing, tables[0], tables[2]))
    rows, where = lax.optimization_barrier((exchange(outgoing.reshape(PEERS, LANES, D)), where))
    rows, partial = score_kept(me, rows, tables)
    for iteration in range(ITERS):
        returned = exchange(score_far(me, rows, tables, partial))
        lse, outward = home(returned, *where)
        inward = exchange(outward)
        last = iteration == ITERS - 1
        if last:
            far = weigh_others(me, rows, tables, (1,), inward)
            arrived = shifted(far[0], 2)
            far, inward = lax.optimization_barrier((far, inward))
            near = weigh_others(me, rows, tables, (0, 2), inward)
        else:
            near = weigh_others(me, rows, tables, (0, 1, 2), inward)
            arrived = shifted(near[1], 2)
        near_arrived = [shifted(near[0], 1), shifted(near[-1], 3)]
        near, inward = lax.optimization_barrier((near, inward))
        own_sum, own_mass = merge(*weigh_own(me, rows, tables, inward), arrived)
        own = finish(own_sum, own_mass, near_arrived, own, (COPIES,) if last else ())
        if not last:
            tables = tables_of(own)
            partial = score_near(me, rows, tables)
    gathered = lax.all_to_all(own, "x", split_axis=0, concat_axis=0, tiled=True)
    return gathered.reshape(COPIES * CB, D), lse[:, :PB].reshape(-1)


def solution(mesh):
    split = Mesh(mesh.devices.reshape(4, 2, 4, 2, 4), ("zh", "zl", "y", "core", "x"))
    pts = ("zh", "zl", "y", "core")
    return jax.shard_map(
        on_device,
        mesh=split,
        in_specs=(P((*pts, "x"), None), P(pts, None), P((*pts, "x"), None)),
        out_specs=(P(pts, None), P((*pts, "x"))),
        check_vma=False,
    )
```

```python
import functools
import math

import jax
import jax.numpy as jnp
from jax import lax
from jax.experimental import pallas as pl
from jax.experimental.pallas import tpu as pltpu
from jax.sharding import Mesh, PartitionSpec as P

D = 512
CB = 256
PB = 16
PBD = 128
NCB = 256
ITERS = 2
CAP = 2
COPIES = 4
PEERS = NCB // COPIES
LANES = COPIES * CAP * PB
SLOTS = PEERS * COPIES * CAP
ENTRIES = 2 * PBD
COLS = PEERS * CAP * PB
MSG = CB + 16
LIMIT = 28
QUARTERS = 4
EMPTY = 1e30
GROUP = ("zl", "y", "core", "x")
BETA = 1.0 / math.sqrt(D)
LOG2E = 1.0 / math.log(2.0)
LN2 = math.log(2.0)
F32 = jnp.float32
BF16 = jnp.bfloat16


def picked_sum(chosen, values):
    total = None
    for _ in range(3):
        piece = values.astype(BF16)
        part = jnp.dot(chosen, piece, preferred_element_type=F32)
        total = part if total is None else total + part
        values = values - piece.astype(F32)
    return total


def iota(shape, dim):
    return lax.broadcasted_iota(jnp.int32, shape, dim)


def pack_kernel(src, points, out):
    base = pl.program_id(0) * out.shape[0]

    def body(i, carry):
        s = src[base + i]
        block = points[jnp.maximum(s, 0)]
        out[i] = jnp.where(s >= 0, block, jnp.zeros_like(block))
        return carry

    lax.fori_loop(0, out.shape[0], body, 0, unroll=8)


def pack(src, points):
    per = 128
    return pl.pallas_call(
        pack_kernel,
        grid_spec=pltpu.PrefetchScalarGridSpec(
            num_scalar_prefetch=1,
            grid=(SLOTS // per,),
            in_specs=[pl.BlockSpec((PBD, PB, D), lambda i, s: (0, 0, 0))],
            out_specs=pl.BlockSpec((per, PB, D), lambda i, s: (i, 0, 0)),
        ),
        out_shape=jax.ShapeDtypeStruct((SLOTS, PB, D), BF16),
        compiler_params=pltpu.CompilerParams(vmem_limit_bytes=58 << 20),
        name="pack_points",
    )(src, points)


def norms_of(table):
    wide = table[...].astype(F32)
    return (BETA * LOG2E) * jnp.sum(wide * wide, axis=1, keepdims=True)


def scores_of(table, block, norms):
    products = lax.dot_general(table[...], block, (((1,), (1,)), ((), ())), preferred_element_type=F32)
    return (2.0 * BETA * LOG2E) * products - norms


def turned_by(value, groups, per_row):
    row = iota(value.shape, 0) % COPIES
    turned = value
    for k in range(COPIES):
        turn = lax.rem(groups + per_row * k + 2 * COPIES, COPIES) * (CAP * PB)
        turned = jnp.where(row == k, pltpu.roll(value, turn, 1), turned)
    return turned


def label_of(me, s):
    return lax.rem(me + 1 + s, COPIES)


def call_whole(kernel, me, rows, tables, which, extra, outs, flops, name):
    return pl.pallas_call(
        functools.partial(kernel, which),
        in_specs=[pl.BlockSpec(memory_space=pltpu.SMEM)]
        + [pl.BlockSpec(memory_space=pltpu.VMEM)] * (1 + len(which) + len(extra)),
        out_shape=outs,
        compiler_params=pltpu.CompilerParams(vmem_limit_bytes=LIMIT << 20),
        name=name,
    )(me, rows, *[tables[s] for s in which], *extra)


def rows_of(rows, label):
    part = rows[:, pl.ds(pl.multiple_of(label * (CAP * PB), CAP * PB), CAP * PB), :]
    return part.reshape(COLS, D)


def scored(total, table, norms, block, label):
    scores = scores_of(table, block, norms)
    highest = jnp.max(scores, axis=0, keepdims=True)
    partial = highest + jnp.log2(jnp.sum(jnp.exp2(scores - highest), axis=0, keepdims=True))
    partial = partial * LN2
    tiles = [jnp.broadcast_to(partial[:, c : c + LANES], (COPIES, LANES)) for c in range(0, block.shape[0], LANES)]
    lanes = iota(total.shape, 1) // (CAP * PB)
    return jnp.where(lanes == label, turned_by(jnp.concatenate(tiles, axis=0), label, -1), total)


def score_kernel(which, me, rows, *refs):
    tables, previous, out = refs[: len(which)], refs[len(which) : -1], refs[-1]
    total = previous[0][...] if previous else jnp.zeros((PEERS, LANES), F32)
    for k, s in enumerate(which):
        label = label_of(me[0], s)
        total = scored(total, tables[k], norms_of(tables[k]), rows_of(rows, label), label)
    out[...] = total


def keep_kernel(which, me, source, *refs):
    tables, (kept, out, done) = refs[: len(which)], refs[len(which) :]
    per = PEERS // QUARTERS
    parts = [pl.ds(i * per, per) for i in range(QUARTERS)]
    copies = [pltpu.make_async_copy(source.at[p], kept.at[p], done.at[i]) for i, p in enumerate(parts)]
    for copy in copies:
        copy.start()
    norms = [norms_of(table) for table in tables]
    for copy, part in zip(copies, parts):
        copy.wait()
        total = jnp.zeros((per, LANES), F32)
        for k, s in enumerate(which):
            label = label_of(me[0], s)
            width = CAP * PB
            block = kept[part, pl.ds(pl.multiple_of(label * width, width), width), :]
            total = scored(total, tables[k], norms[k], block.reshape(per * width, D), label)
        out[part, :] = total


def score_kept(me, received, tables):
    which = (0, 2, 3)
    vmem = pl.BlockSpec(memory_space=pltpu.VMEM)
    return pl.pallas_call(
        functools.partial(keep_kernel, which),
        in_specs=[pl.BlockSpec(memory_space=pltpu.SMEM), pl.BlockSpec(memory_space=pl.ANY)] + [vmem] * len(which),
        out_specs=(vmem, vmem),
        out_shape=(
            jax.ShapeDtypeStruct(received.shape, received.dtype),
            jax.ShapeDtypeStruct((PEERS, LANES), F32),
        ),
        scratch_shapes=[pltpu.SemaphoreType.DMA((QUARTERS,))],
        compiler_params=pltpu.CompilerParams(vmem_limit_bytes=LIMIT << 20),
        name="keep_and_score",
    )(me, received, *[tables[s] for s in which])


def score_near(me, rows, tables):
    out = jax.ShapeDtypeStruct((PEERS, LANES), F32)
    return call_whole(score_kernel, me, rows, tables, (0, 2, 3), (), out, 2, "score_near")


def score_far(me, rows, tables, partial):
    out = jax.ShapeDtypeStruct((PEERS, LANES), F32)
    return call_whole(score_kernel, me, rows, tables, (1,), (partial,), out, 2, "score_far")


def home_kernel(returned, peer_col, slot_col, peer_row, lse, outward):
    pick = (iota((ENTRIES, PEERS), 1) == peer_col[...]).astype(BF16)
    mask = (iota((ENTRIES, LANES), 1) // PB == slot_col[...]).astype(F32)
    mine = picked_sum(pick, returned[...]) * mask
    turn = LANES // 2
    while turn >= PB:
        mine = mine + pltpu.roll(mine, turn, 1)
        turn //= 2
    first, second = mine[:PBD], mine[PBD:]
    highest = jnp.maximum(first, second)
    total = highest + jnp.log(jnp.exp(first - highest) + jnp.exp(second - highest))
    lse[...] = total
    place = (iota((PEERS, ENTRIES), 0) == peer_row[...]).astype(BF16)
    filled = jnp.dot(place, mask.astype(BF16), preferred_element_type=F32)
    both = jnp.concatenate([total, total], axis=0)
    outward[...] = jnp.where(filled > 0.5, picked_sum(place, both * mask), EMPTY)


def home(returned, peer_col, slot_col, peer_row):
    return pl.pallas_call(
        home_kernel,
        out_shape=(
            jax.ShapeDtypeStruct((PBD, LANES), F32),
            jax.ShapeDtypeStruct((PEERS, LANES), F32),
        ),
        compiler_params=pltpu.CompilerParams(vmem_limit_bytes=8 << 20),
        name="join_halves",
    )(returned, peer_col, slot_col, peer_row)


def weigh_kernel(which, me, rows, *refs):
    tables, inward, outs = refs[: len(which)], refs[len(which)], refs[len(which) + 1 :]
    mine = iota((PEERS, LANES), 1) // (CAP * PB) == iota((PEERS, LANES), 0) % COPIES
    incoming = inward[...] * LOG2E
    for k, s in enumerate(which):
        label = label_of(me[0], s)
        block = rows_of(rows, label)
        turned = jnp.where(mine, turned_by(incoming, -label, 1), 0.0)
        tiles = [jnp.sum(turned[c : c + COPIES], axis=0, keepdims=True) for c in range(0, PEERS, COPIES)]
        point_lse = jnp.concatenate(tiles, axis=1)
        weights = jnp.exp2(scores_of(tables[k], block, norms_of(tables[k])) - point_lse)
        sums = jnp.dot(weights.astype(BF16), block, preferred_element_type=F32)
        mass = weights[:, :128]
        for c in range(128, COLS, 128):
            mass += weights[:, c : c + 128]
        mass = jnp.sum(mass.T, axis=0, keepdims=True)
        if s == COPIES - 1:
            outs[0][...] = sums
            outs[1][...] = jnp.broadcast_to(mass, outs[1].shape)
            continue
        coarse = mass.astype(BF16).astype(F32)
        fine = mass - coarse
        outs[0][k, :CB] = sums.astype(BF16)
        pair = jnp.concatenate([coarse, fine], axis=1)
        outs[0][k, CB:] = jnp.broadcast_to(pair, (MSG - CB, D)).astype(BF16)


def weigh_own(me, rows, tables, inward):
    outs = (jax.ShapeDtypeStruct((CB, D), F32), jax.ShapeDtypeStruct((8, CB), F32))
    return call_whole(weigh_kernel, me, rows, tables, (3,), (inward,), outs, 4, "weigh_own")


def weigh_others(me, rows, tables, which, inward):
    out = jax.ShapeDtypeStruct((len(which), MSG, D), BF16)
    return call_whole(weigh_kernel, me, rows, tables, which, (inward,), out, 4, "weigh_others")


def merge_kernel(own_sum, own_mass, message, total, mass):
    total[...] = own_sum[...] + message[:CB].astype(F32)
    pair = message[CB:].astype(F32)[:1]
    mass[...] = own_mass[...] + pair[:, :CB] + pair[:, CB:]


def merge(own_sum, own_mass, message):
    return pl.pallas_call(
        merge_kernel,
        out_shape=(jax.ShapeDtypeStruct((CB, D), F32), jax.ShapeDtypeStruct((8, CB), F32)),
        compiler_params=pltpu.CompilerParams(vmem_limit_bytes=16 << 20),
        name="merge_far",
    )(own_sum, own_mass, message)


def finish_kernel(own_sum, own_mass, m1, m2, table, out):
    total, mass = own_sum[...], own_mass[:1]
    for message in (m1, m2):
        total += message[:CB].astype(F32)
        pair = message[CB:].astype(F32)[:1]
        mass += pair[:, :CB] + pair[:, CB:]
    column = jnp.broadcast_to(mass + 1.0, (128, CB)).T[:, :1]
    out[...] = ((total + table[...].astype(F32)) / column).astype(BF16)


def finish(own_sum, own_mass, arrived, table):
    return pl.pallas_call(
        finish_kernel,
        out_shape=jax.ShapeDtypeStruct((CB, D), BF16),
        compiler_params=pltpu.CompilerParams(vmem_limit_bytes=16 << 20),
        name="new_centres",
    )(own_sum, own_mass, *arrived, table)


def place_kernel(x, *refs):
    pieces, out = refs[:-1], refs[-1]
    for n in range(COPIES):
        out[lax.rem(x[0] + COPIES - n, COPIES)] = pieces[n][...]


def place(x, pieces):
    return pl.pallas_call(
        place_kernel,
        in_specs=[pl.BlockSpec(memory_space=pltpu.SMEM)] + [pl.BlockSpec(memory_space=pltpu.VMEM)] * COPIES,
        out_shape=jax.ShapeDtypeStruct((COPIES, CB, D), BF16),
        compiler_params=pltpu.CompilerParams(vmem_limit_bytes=16 << 20),
        name="place_blocks",
    )(x, *pieces)


def shifted(value, by, axis="zh"):
    return lax.ppermute(value, axis, [(i, (i + by) % COPIES) for i in range(COPIES)])


def tables_of(own):
    return [shifted(own, COPIES - 1 - s) for s in range(COPIES - 1)] + [own]


def exchange(value):
    return lax.all_to_all(value, GROUP, split_axis=0, concat_axis=0, tiled=True)


def route(candidates):
    picked = candidates.T.reshape(-1)
    labels = jnp.arange(NCB, dtype=jnp.int32)
    member = (picked[:, None] == labels[None, :]).astype(BF16)
    index = jnp.arange(ENTRIES, dtype=jnp.int32)
    earlier = (index[None, :] < index[:, None]).astype(BF16)
    hits = jnp.dot(earlier, member, preferred_element_type=F32)
    arrival = jnp.sum(hits * member.astype(F32), axis=1).astype(jnp.int32)
    peer = picked % PEERS
    slot = picked // PEERS * CAP + arrival
    position = peer * (COPIES * CAP) + slot
    places = jnp.arange(SLOTS, dtype=jnp.int32)
    source = jnp.sum(jnp.where(position[:, None] == places[None, :], index[:, None] % PBD + 1, 0), axis=0) - 1
    return source, peer, slot


def on_device(points, centroids, candidates):
    me = lax.axis_index("zh").reshape(1)
    own = lax.dynamic_slice_in_dim(centroids, lax.axis_index("x") * CB, CB, 0)
    source, peer, slot = route(candidates)
    outgoing = pack(source, points.reshape(PBD, PB, D))
    where = (peer[:, None], slot[:, None], peer[None, :])
    tables = tables_of(own)
    outgoing, tables[0], tables[2] = lax.optimization_barrier((outgoing, tables[0], tables[2]))
    rows, where = lax.optimization_barrier((exchange(outgoing.reshape(PEERS, LANES, D)), where))
    rows, partial = score_kept(me, rows, tables)
    for iteration in range(ITERS):
        returned = exchange(score_far(me, rows, tables, partial))
        lse, outward = home(returned, *where)
        inward = exchange(outward)
        last = iteration == ITERS - 1
        if last:
            far = weigh_others(me, rows, tables, (1,), inward)
            arrived = shifted(far[0], 2)
            far, inward = lax.optimization_barrier((far, inward))
            near = weigh_others(me, rows, tables, (0, 2), inward)
        else:
            near = weigh_others(me, rows, tables, (0, 1, 2), inward)
            arrived = shifted(near[1], 2)
        near_arrived = [shifted(near[0], 1), shifted(near[-1], 3)]
        near, inward = lax.optimization_barrier((near, inward))
        own_sum, own_mass = merge(*weigh_own(me, rows, tables, inward), arrived)
        own = finish(own_sum, own_mass, near_arrived, own)
        if not last:
            tables = tables_of(own)
            partial = score_near(me, rows, tables)
    pieces = [own] + [shifted(own, n, "x") for n in (1, 2, 3)]
    gathered = place(lax.axis_index("x").reshape(1), pieces)
    return gathered.reshape(COPIES * CB, D), lse[:, :PB].reshape(-1)


def solution(mesh):
    split = Mesh(mesh.devices.reshape(4, 2, 4, 2, 4), ("zh", "zl", "y", "core", "x"))
    pts = ("zh", "zl", "y", "core")
    return jax.shard_map(
        on_device,
        mesh=split,
        in_specs=(P((*pts, "x"), None), P(pts, None), P((*pts, "x"), None)),
        out_specs=(P(pts, None), P((*pts, "x"))),
        check_vma=False,
    )
```

```python
import functools
import math

import jax
import jax.numpy as jnp
from jax import lax
from jax.experimental import pallas as pl
from jax.experimental.pallas import tpu as pltpu
from jax.sharding import Mesh, PartitionSpec as P

D = 512
CB = 256
PB = 16
PBD = 128
NCB = 256
ITERS = 2
CAP = 2
COPIES = 4
PEERS = NCB // COPIES
LANES = COPIES * CAP * PB
SLOTS = PEERS * COPIES * CAP
ENTRIES = 2 * PBD
COLS = PEERS * CAP * PB
MSG = CB + 16
LIMIT = 28
QUARTERS = 4
EMPTY = 1e30
GROUP = ("zl", "y", "core", "x")
BETA = 1.0 / math.sqrt(D)
LOG2E = 1.0 / math.log(2.0)
LN2 = math.log(2.0)
F32 = jnp.float32
BF16 = jnp.bfloat16


def picked_sum(chosen, values):
    total = None
    for _ in range(3):
        piece = values.astype(BF16)
        part = jnp.dot(chosen, piece, preferred_element_type=F32)
        total = part if total is None else total + part
        values = values - piece.astype(F32)
    return total


def iota(shape, dim):
    return lax.broadcasted_iota(jnp.int32, shape, dim)


def fetch_kernel(x, source, out, done):
    start = pl.multiple_of(x[0] * CB, CB)
    copy = pltpu.make_async_copy(source.at[pl.ds(start, CB)], out, done)
    copy.start()
    copy.wait()


def fetch(x, centroids):
    return pl.pallas_call(
        fetch_kernel,
        in_specs=[pl.BlockSpec(memory_space=pltpu.SMEM), pl.BlockSpec(memory_space=pl.ANY)],
        out_specs=pl.BlockSpec(memory_space=pltpu.VMEM),
        out_shape=jax.ShapeDtypeStruct((CB, D), BF16),
        scratch_shapes=[pltpu.SemaphoreType.DMA],
        compiler_params=pltpu.CompilerParams(vmem_limit_bytes=58 << 20),
        name="fetch_own",
    )(x, centroids)


def pack_kernel(src, points, out):
    base = pl.program_id(0) * out.shape[0]

    def body(i, carry):
        s = src[base + i]
        block = points[jnp.maximum(s, 0)]
        out[i] = jnp.where(s >= 0, block, jnp.zeros_like(block))
        return carry

    lax.fori_loop(0, out.shape[0], body, 0, unroll=8)


def pack(src, points):
    per = 128
    return pl.pallas_call(
        pack_kernel,
        grid_spec=pltpu.PrefetchScalarGridSpec(
            num_scalar_prefetch=1,
            grid=(SLOTS // per,),
            in_specs=[pl.BlockSpec((PBD, PB, D), lambda i, s: (0, 0, 0))],
            out_specs=pl.BlockSpec((per, PB, D), lambda i, s: (i, 0, 0)),
        ),
        out_shape=jax.ShapeDtypeStruct((SLOTS, PB, D), BF16),
        compiler_params=pltpu.CompilerParams(vmem_limit_bytes=58 << 20),
        name="pack_points",
    )(src, points)


def norms_of(table):
    wide = table[...].astype(F32)
    return (BETA * LOG2E) * jnp.sum(wide * wide, axis=1, keepdims=True)


def scores_of(table, block, norms):
    products = lax.dot_general(table[...], block, (((1,), (1,)), ((), ())), preferred_element_type=F32)
    return (2.0 * BETA * LOG2E) * products - norms


def turned_by(value, groups, per_row):
    row = iota(value.shape, 0) % COPIES
    turned = value
    for k in range(COPIES):
        turn = lax.rem(groups + per_row * k + 2 * COPIES, COPIES) * (CAP * PB)
        turned = jnp.where(row == k, pltpu.roll(value, turn, 1), turned)
    return turned


def label_of(me, s):
    return lax.rem(me + 1 + s, COPIES)


def call_whole(kernel, me, rows, tables, which, extra, outs, flops, name):
    return pl.pallas_call(
        functools.partial(kernel, which),
        in_specs=[pl.BlockSpec(memory_space=pltpu.SMEM)]
        + [pl.BlockSpec(memory_space=pltpu.VMEM)] * (1 + len(which) + len(extra)),
        out_shape=outs,
        compiler_params=pltpu.CompilerParams(vmem_limit_bytes=LIMIT << 20),
        name=name,
    )(me, rows, *[tables[s] for s in which], *extra)


def rows_of(rows, label):
    part = rows[:, pl.ds(pl.multiple_of(label * (CAP * PB), CAP * PB), CAP * PB), :]
    return part.reshape(COLS, D)


def scored(total, table, norms, block, label):
    scores = scores_of(table, block, norms)
    highest = jnp.max(scores, axis=0, keepdims=True)
    partial = highest + jnp.log2(jnp.sum(jnp.exp2(scores - highest), axis=0, keepdims=True))
    partial = partial * LN2
    tiles = [jnp.broadcast_to(partial[:, c : c + LANES], (COPIES, LANES)) for c in range(0, block.shape[0], LANES)]
    lanes = iota(total.shape, 1) // (CAP * PB)
    return jnp.where(lanes == label, turned_by(jnp.concatenate(tiles, axis=0), label, -1), total)


def score_kernel(which, me, rows, *refs):
    tables, previous, out = refs[: len(which)], refs[len(which) : -1], refs[-1]
    total = previous[0][...] if previous else jnp.zeros((PEERS, LANES), F32)
    for k, s in enumerate(which):
        label = label_of(me[0], s)
        total = scored(total, tables[k], norms_of(tables[k]), rows_of(rows, label), label)
    out[...] = total


def keep_kernel(which, me, source, *refs):
    tables, (kept, out, done) = refs[: len(which)], refs[len(which) :]
    per = PEERS // QUARTERS
    parts = [pl.ds(i * per, per) for i in range(QUARTERS)]
    copies = [pltpu.make_async_copy(source.at[p], kept.at[p], done.at[i]) for i, p in enumerate(parts)]
    for copy in copies:
        copy.start()
    norms = [norms_of(table) for table in tables]
    for copy, part in zip(copies, parts):
        copy.wait()
        total = jnp.zeros((per, LANES), F32)
        for k, s in enumerate(which):
            label = label_of(me[0], s)
            width = CAP * PB
            block = kept[part, pl.ds(pl.multiple_of(label * width, width), width), :]
            total = scored(total, tables[k], norms[k], block.reshape(per * width, D), label)
        out[part, :] = total


def score_kept(me, received, tables):
    which = (0, 2, 3)
    vmem = pl.BlockSpec(memory_space=pltpu.VMEM)
    return pl.pallas_call(
        functools.partial(keep_kernel, which),
        in_specs=[pl.BlockSpec(memory_space=pltpu.SMEM), pl.BlockSpec(memory_space=pl.ANY)] + [vmem] * len(which),
        out_specs=(vmem, vmem),
        out_shape=(
            jax.ShapeDtypeStruct(received.shape, received.dtype),
            jax.ShapeDtypeStruct((PEERS, LANES), F32),
        ),
        scratch_shapes=[pltpu.SemaphoreType.DMA((QUARTERS,))],
        compiler_params=pltpu.CompilerParams(vmem_limit_bytes=LIMIT << 20),
        name="keep_and_score",
    )(me, received, *[tables[s] for s in which])


def score_near(me, rows, tables):
    out = jax.ShapeDtypeStruct((PEERS, LANES), F32)
    return call_whole(score_kernel, me, rows, tables, (0, 2, 3), (), out, 2, "score_near")


def score_far(me, rows, tables, partial):
    out = jax.ShapeDtypeStruct((PEERS, LANES), F32)
    return call_whole(score_kernel, me, rows, tables, (1,), (partial,), out, 2, "score_far")


def home_kernel(returned, peer_col, slot_col, peer_row, lse, outward):
    pick = (iota((ENTRIES, PEERS), 1) == peer_col[...]).astype(BF16)
    mask = (iota((ENTRIES, LANES), 1) // PB == slot_col[...]).astype(F32)
    mine = picked_sum(pick, returned[...]) * mask
    turn = LANES // 2
    while turn >= PB:
        mine = mine + pltpu.roll(mine, turn, 1)
        turn //= 2
    first, second = mine[:PBD], mine[PBD:]
    highest = jnp.maximum(first, second)
    total = highest + jnp.log(jnp.exp(first - highest) + jnp.exp(second - highest))
    lse[...] = total
    place = (iota((PEERS, ENTRIES), 0) == peer_row[...]).astype(BF16)
    filled = jnp.dot(place, mask.astype(BF16), preferred_element_type=F32)
    both = jnp.concatenate([total, total], axis=0)
    outward[...] = jnp.where(filled > 0.5, picked_sum(place, both * mask), EMPTY)


def home(returned, peer_col, slot_col, peer_row):
    return pl.pallas_call(
        home_kernel,
        out_shape=(
            jax.ShapeDtypeStruct((PBD, LANES), F32),
            jax.ShapeDtypeStruct((PEERS, LANES), F32),
        ),
        compiler_params=pltpu.CompilerParams(vmem_limit_bytes=8 << 20),
        name="join_halves",
    )(returned, peer_col, slot_col, peer_row)


def weigh_kernel(which, me, rows, *refs):
    tables, inward, outs = refs[: len(which)], refs[len(which)], refs[len(which) + 1 :]
    mine = iota((PEERS, LANES), 1) // (CAP * PB) == iota((PEERS, LANES), 0) % COPIES
    incoming = inward[...] * LOG2E
    for k, s in enumerate(which):
        label = label_of(me[0], s)
        block = rows_of(rows, label)
        turned = jnp.where(mine, turned_by(incoming, -label, 1), 0.0)
        tiles = [jnp.sum(turned[c : c + COPIES], axis=0, keepdims=True) for c in range(0, PEERS, COPIES)]
        point_lse = jnp.concatenate(tiles, axis=1)
        weights = jnp.exp2(scores_of(tables[k], block, norms_of(tables[k])) - point_lse)
        sums = jnp.dot(weights.astype(BF16), block, preferred_element_type=F32)
        mass = weights[:, :128]
        for c in range(128, COLS, 128):
            mass += weights[:, c : c + 128]
        mass = jnp.sum(mass.T, axis=0, keepdims=True)
        if s == COPIES - 1:
            outs[0][...] = sums
            outs[1][...] = jnp.broadcast_to(mass, outs[1].shape)
            continue
        coarse = mass.astype(BF16).astype(F32)
        fine = mass - coarse
        outs[0][k, :CB] = sums.astype(BF16)
        pair = jnp.concatenate([coarse, fine], axis=1)
        outs[0][k, CB:] = jnp.broadcast_to(pair, (MSG - CB, D)).astype(BF16)


def weigh_own(me, rows, tables, inward):
    outs = (jax.ShapeDtypeStruct((CB, D), F32), jax.ShapeDtypeStruct((8, CB), F32))
    return call_whole(weigh_kernel, me, rows, tables, (3,), (inward,), outs, 4, "weigh_own")


def weigh_others(me, rows, tables, which, inward):
    out = jax.ShapeDtypeStruct((len(which), MSG, D), BF16)
    return call_whole(weigh_kernel, me, rows, tables, which, (inward,), out, 4, "weigh_others")


def merge_kernel(own_sum, own_mass, message, total, mass):
    total[...] = own_sum[...] + message[:CB].astype(F32)
    pair = message[CB:].astype(F32)[:1]
    mass[...] = own_mass[...] + pair[:, :CB] + pair[:, CB:]


def merge(own_sum, own_mass, message):
    return pl.pallas_call(
        merge_kernel,
        out_shape=(jax.ShapeDtypeStruct((CB, D), F32), jax.ShapeDtypeStruct((8, CB), F32)),
        compiler_params=pltpu.CompilerParams(vmem_limit_bytes=16 << 20),
        name="merge_far",
    )(own_sum, own_mass, message)


def finish_kernel(own_sum, own_mass, m1, m2, table, out):
    total, mass = own_sum[...], own_mass[:1]
    for message in (m1, m2):
        total += message[:CB].astype(F32)
        pair = message[CB:].astype(F32)[:1]
        mass += pair[:, :CB] + pair[:, CB:]
    column = jnp.broadcast_to(mass + 1.0, (128, CB)).T[:, :1]
    out[...] = ((total + table[...].astype(F32)) / column).astype(BF16)


def finish(own_sum, own_mass, arrived, table):
    return pl.pallas_call(
        finish_kernel,
        out_shape=jax.ShapeDtypeStruct((CB, D), BF16),
        compiler_params=pltpu.CompilerParams(vmem_limit_bytes=16 << 20),
        name="new_centres",
    )(own_sum, own_mass, *arrived, table)


def place_kernel(x, *refs):
    pieces, out = refs[:-1], refs[-1]
    for n in range(COPIES):
        out[lax.rem(x[0] + COPIES - n, COPIES)] = pieces[n][...]


def place(x, pieces):
    return pl.pallas_call(
        place_kernel,
        in_specs=[pl.BlockSpec(memory_space=pltpu.SMEM)] + [pl.BlockSpec(memory_space=pltpu.VMEM)] * COPIES,
        out_shape=jax.ShapeDtypeStruct((COPIES, CB, D), BF16),
        compiler_params=pltpu.CompilerParams(vmem_limit_bytes=16 << 20),
        name="place_blocks",
    )(x, *pieces)


def shifted(value, by, axis="zh"):
    return lax.ppermute(value, axis, [(i, (i + by) % COPIES) for i in range(COPIES)])


def tables_of(own):
    return [shifted(own, COPIES - 1 - s) for s in range(COPIES - 1)] + [own]


def exchange(value):
    return lax.all_to_all(value, GROUP, split_axis=0, concat_axis=0, tiled=True)


def route(candidates):
    picked = candidates.T.reshape(-1)
    labels = jnp.arange(NCB, dtype=jnp.int32)
    member = (picked[:, None] == labels[None, :]).astype(BF16)
    index = jnp.arange(ENTRIES, dtype=jnp.int32)
    earlier = (index[None, :] < index[:, None]).astype(BF16)
    hits = jnp.dot(earlier, member, preferred_element_type=F32)
    arrival = jnp.sum(hits * member.astype(F32), axis=1).astype(jnp.int32)
    peer = picked % PEERS
    slot = picked // PEERS * CAP + arrival
    position = peer * (COPIES * CAP) + slot
    places = jnp.arange(SLOTS, dtype=jnp.int32)
    source = jnp.sum(jnp.where(position[:, None] == places[None, :], index[:, None] % PBD + 1, 0), axis=0) - 1
    return source, peer, slot


def on_device(points, centroids, candidates):
    me = lax.axis_index("zh").reshape(1)
    own = fetch(lax.axis_index("x").reshape(1), centroids)
    source, peer, slot = route(candidates)
    outgoing = pack(source, points.reshape(PBD, PB, D))
    where = (peer[:, None], slot[:, None], peer[None, :])
    tables = tables_of(own)
    outgoing, tables[0], tables[2] = lax.optimization_barrier((outgoing, tables[0], tables[2]))
    rows, where = lax.optimization_barrier((exchange(outgoing.reshape(PEERS, LANES, D)), where))
    rows, partial = score_kept(me, rows, tables)
    for iteration in range(ITERS):
        returned = exchange(score_far(me, rows, tables, partial))
        lse, outward = home(returned, *where)
        inward = exchange(outward)
        last = iteration == ITERS - 1
        if last:
            far = weigh_others(me, rows, tables, (1,), inward)
            arrived = shifted(far[0], 2)
            far, inward = lax.optimization_barrier((far, inward))
            near = weigh_others(me, rows, tables, (0, 2), inward)
        else:
            near = weigh_others(me, rows, tables, (0, 1, 2), inward)
            arrived = shifted(near[1], 2)
        near_arrived = [shifted(near[0], 1), shifted(near[-1], 3)]
        near, inward = lax.optimization_barrier((near, inward))
        own_sum, own_mass = merge(*weigh_own(me, rows, tables, inward), arrived)
        own = finish(own_sum, own_mass, near_arrived, own)
        if not last:
            tables = tables_of(own)
            partial = score_near(me, rows, tables)
    pieces = [own] + [shifted(own, n, "x") for n in (1, 2, 3)]
    gathered = place(lax.axis_index("x").reshape(1), pieces)
    return gathered.reshape(COPIES * CB, D), lse[:, :PB].reshape(-1)


def solution(mesh):
    split = Mesh(mesh.devices.reshape(4, 2, 4, 2, 4), ("zh", "zl", "y", "core", "x"))
    pts = ("zh", "zl", "y", "core")
    return jax.shard_map(
        on_device,
        mesh=split,
        in_specs=(P((*pts, "x"), None), P(pts, None), P((*pts, "x"), None)),
        out_specs=(P(pts, None), P((*pts, "x"))),
        check_vma=False,
    )
```
